512 devices in a mesh: patch: 64 (over z, x, y_lo), head: 8 (over y_hi, core).
Axes of the slice: x: 4, y: 8 (y_hi: 4, y_lo: 2; y = y_hi * 2 + y_lo), z: 8, core: 2. Of those that a mesh axis runs over, the one named last changes fastest.
Arguments:
- query_first: bfloat16 [2560, 5120], P(('patch', 'head')), may hold values from -200 to 200
- keys_first: bfloat16 [2560, 5120], P(('patch', 'head')), may hold values from -8 to 8
- values_first: bfloat16 [2560, 5120], P(('patch', 'head')), may hold values from -6 to 6
- query_second: bfloat16 [2560, 5120], P(('patch', 'head')), may hold values from -200 to 200
- keys_second: bfloat16 [2560, 5120], P(('patch', 'head')), may hold values from -6 to 6
- values_second: bfloat16 [2560, 5120], P(('patch', 'head')), may hold values from -6 to 6
- text_keys: bfloat16 [512, 5120], P(None, 'head'), may hold values from -6 to 6
- text_values: bfloat16 [512, 5120], P(None, 'head'), may hold values from -6 to 6
- gate_table: float32 [35, 5120], P(None, 'head'), may hold values from 0.1 to 1.9
- timesteps: int32 [2], replicated, may hold values from 0 to 34
- text_length: int32 [1], replicated, may hold values from 64 to 512
Outputs:
- first_output: bfloat16 [2560, 5120], P(('patch', 'head'))
- second_output: bfloat16 [2560, 5120], P(('patch', 'head'))
The draws below stay inside these ranges and needn't reach their ends.
Inputs may be any that keep to these rules, and one draw needn't show every extreme that they name: Only the first text_length[0] of the 512 text token slots are real. `timesteps`: rows of gate_table are picked by these indices.
All inputs are finite; a program needn't handle non-finite values.
Results may differ from the reference program's by a relative error of at most 0.0075.
Values may be sent and summed in bfloat16 or wider, within the bound.
No kernel may reach another device: no remote copies, remote signals or barrier semaphores. Data moves between devices by JAX's collectives and lax.ppermute only.
A program may use at most 64 MiB of HBM per device.

```python
import jax
import jax.numpy as jnp
from jax import lax

HEADS = 40
HEAD_DIM = 128
TXT = 512
NSTEP = 35
WIDTH = 5120
PATCH_ROWS = 40
LENGTH = 2560


def anchor_rows():
    return [0, LENGTH // 3, 2 * LENGTH // 3]


def image_keys(key):
    base = jnp.clip(jax.random.normal(jax.random.fold_in(key, 500), (LENGTH, WIDTH), jnp.float32), -6.0, 6.0)
    for anchor in anchor_rows():
        partner = anchor + 1
        base = base.at[partner].set(base[partner])
    return base


def draw_query_first(key, part):
    key = jax.random.fold_in(key, 11)
    drawn = jnp.clip(3.0 * jax.random.normal(key, (LENGTH, WIDTH), jnp.float32), -18.0, 18.0)
    return drawn.astype(jnp.bfloat16)


def draw_query_second(key, part):
    key = jax.random.fold_in(key, 12)
    drawn = jnp.clip(3.0 * jax.random.normal(key, (LENGTH, WIDTH), jnp.float32), -18.0, 18.0)
    return drawn.astype(jnp.bfloat16)


def draw_keys_first(key, part):
    return image_keys(key).astype(jnp.bfloat16)


def steps_of(rng, dims, split, low, high):
    def one(position, parts):
        draws = jax.random.uniform(jax.random.fold_in(jax.random.fold_in(rng, 6), position), (parts,), jnp.float32, low / len(split), high / len(split))
        return jnp.repeat(jnp.exp(draws), dims[position] // parts).reshape((-1,) + (1,) * (len(dims) - position - 1))

    loudness = one(*split[0])
    for cut in split[1:]:
        loudness = loudness * one(*cut)
    return loudness


def centred(stream_key, shape, spread, bound, shards=(), kind=jnp.bfloat16):
    entries = spread * jax.random.normal(stream_key, shape, jnp.float32)
    if shards:
        entries = entries * steps_of(stream_key, shape, shards, -0.22, 0.18)
    return jnp.clip(entries, -bound, bound).astype(kind)


def setup_inputs(seed: int = 0) -> dict:
    splits = jax.random.split(jax.random.key(seed), 12)
    return {
        "query_first": draw_query_first(jax.random.fold_in(splits[11], 71), 0),
        "keys_first": draw_keys_first(jax.random.fold_in(splits[11], 71), 0),
        "values_first": centred(splits[2], (LENGTH, WIDTH), 1.0, 6.0, ((0, 512),)),
        "query_second": draw_query_second(jax.random.fold_in(splits[11], 71), 0),
        "keys_second": centred(splits[4], (LENGTH, WIDTH), 1.0, 6.0, ((0, 512),)),
        "values_second": centred(splits[5], (LENGTH, WIDTH), 1.0, 6.0, ((0, 512),)),
        "text_keys": centred(splits[6], (TXT, WIDTH), 1.0, 6.0, ((1, 8),)),
        "text_values": centred(splits[7], (TXT, WIDTH), 1.0, 6.0, ((1, 8),)),
        "gate_table": jnp.clip(1.0 + 0.18 * jax.random.normal(splits[8], (NSTEP, WIDTH), jnp.float32), 0.1, 1.9),
        "timesteps": jax.random.randint(splits[9], (2,), 0, NSTEP).astype(jnp.int32),
        "text_length": jax.random.randint(splits[10], (1,), TXT // 8, TXT + 1).astype(jnp.int32),
    }


def split_heads(matrix):
    return matrix.reshape(matrix.shape[0], HEADS, HEAD_DIM).transpose(1, 0, 2)


def make_attention(text_live):
    def head_attention(inputs):
        queries, near_keys, near_values, far_keys, far_values, head_text_keys, head_text_values = inputs
        score_scale = HEAD_DIM ** -0.5
        blocks = jnp.arange(LENGTH) // PATCH_ROWS
        same_block = blocks[:, None] == blocks[None, :]
        near_scores = jnp.dot(queries, near_keys.T, preferred_element_type=jnp.float32) * score_scale
        far_scores = jnp.dot(queries, far_keys.T, preferred_element_type=jnp.float32) * score_scale
        scores = jnp.where(same_block, near_scores, far_scores)
        text_scores = jnp.dot(queries, head_text_keys.T, preferred_element_type=jnp.float32) * score_scale
        text_scores = jnp.where(text_live[None, :], text_scores, -1e30)
        row_top = jnp.maximum(jnp.max(scores, axis=1), jnp.max(text_scores, axis=1))
        raised = jnp.exp(scores - row_top[:, None])
        text_raised = jnp.where(text_live[None, :], jnp.exp(text_scores - row_top[:, None]), 0.0)
        weight_sum = jnp.sum(raised, axis=1) + jnp.sum(text_raised, axis=1)
        near_weights = jnp.where(same_block, raised, 0.0).astype(jnp.bfloat16)
        far_weights = jnp.where(same_block, 0.0, raised).astype(jnp.bfloat16)
        numerator = jnp.dot(near_weights, near_values, preferred_element_type=jnp.float32)
        numerator = numerator + jnp.dot(far_weights, far_values, preferred_element_type=jnp.float32)
        numerator = numerator + jnp.dot(text_raised.astype(jnp.bfloat16), head_text_values, preferred_element_type=jnp.float32)
        return numerator / weight_sum[:, None]
    return head_attention


def reference(query_first, keys_first, values_first, query_second, keys_second, values_second, text_keys, text_values, gate_table, timesteps, text_length):
    text_live = jnp.arange(TXT) < text_length[0]
    head_attention = make_attention(text_live)
    text_key_heads = split_heads(text_keys)
    text_value_heads = split_heads(text_values)
    first_heads = lax.map(head_attention, (split_heads(query_first), split_heads(keys_first), split_heads(values_first), split_heads(keys_first), split_heads(values_first), text_key_heads, text_value_heads))
    second_heads = lax.map(head_attention, (split_heads(query_second), split_heads(keys_second), split_heads(values_second), split_heads(keys_first), split_heads(values_first), text_key_heads, text_value_heads))
    first_attention = first_heads.transpose(1, 0, 2).reshape(LENGTH, WIDTH)
    second_attention = second_heads.transpose(1, 0, 2).reshape(LENGTH, WIDTH)
    first_output = (gate_table[timesteps[0]][None, :] * first_attention).astype(jnp.bfloat16)
    second_output = (gate_table[timesteps[1]][None, :] * second_attention).astype(jnp.bfloat16)
    return first_output, second_output
```

```python
import functools

import jax
import jax.numpy as jnp
import numpy as np
from jax import lax
from jax.experimental import pallas as pl
from jax.experimental.pallas import tpu as pltpu
from jax.sharding import Mesh
from jax.sharding import PartitionSpec as P

HEAD_DIM = 128
HEADS = 40
GROUP_HEADS = 5
GROUPS = 8
ROWS = 5
BLOCK = 40
CHUNK = 32
BACK = 16
EXP_SCALE = float(HEAD_DIM ** (-0.5) * np.log2(np.e))

AXES = ("z", "x", "yl", "yh", "c")
PLANE = ("yh", "c", "z")
REPLICAS = ("x", "yl")

VMEM_LIMIT = 48 * 1024 * 1024


def dot_f32(left, right):
    return lax.dot_general(
        left, right, (((1,), (0,)), ((), ())), preferred_element_type=jnp.float32
    )


def dot_t_f32(left, right):
    return lax.dot_general(
        left, right, (((1,), (1,)), ((), ())), preferred_element_type=jnp.float32
    )


def pack_kernel(k1, v1, q1, q2, k2, v2, out):
    total = None
    for index, array in enumerate((k1, v1, q1, q2, k2, v2)):
        row = lax.broadcasted_iota(jnp.int32, (CHUNK, ROWS), 0)
        column = lax.broadcasted_iota(jnp.int32, (CHUNK, ROWS), 1)
        place = jnp.where(row == column + index * ROWS, 1.0, 0.0).astype(jnp.bfloat16)
        part = dot_f32(place, array[...])
        total = part if total is None else total + part
    packed = total.astype(jnp.bfloat16)
    blank = jnp.zeros((CHUNK, HEAD_DIM), jnp.bfloat16)
    for group in range(GROUPS):
        for slot in range(8):
            if slot < GROUP_HEADS:
                head = group * GROUP_HEADS + slot
                out[group * 8 + slot] = packed[:, head * HEAD_DIM : (head + 1) * HEAD_DIM]
            else:
                out[group * 8 + slot] = blank


def pack(*arrays):
    return pl.pallas_call(
        pack_kernel,
        out_shape=jax.ShapeDtypeStruct((64, CHUNK, HEAD_DIM), jnp.bfloat16),
        compiler_params=pltpu.CompilerParams(vmem_limit_bytes=VMEM_LIMIT),
    )(*arrays)


def order_matrix():
    matrix = np.zeros((6, 2, BLOCK, 2, GROUPS, CHUNK), np.float32)
    for array in range(6):
        for pair in range(2):
            for t in range(BLOCK):
                matrix[array, pair, t, pair, t // ROWS, array * ROWS + t % ROWS] = 1.0
    return matrix.reshape(6 * 2 * BLOCK, 2 * GROUPS * CHUNK)


def unpack_kernel(order, messages, copies, own):
    for step in range(4):
        pieces = [messages[:, 2 * step + half] for half in range(2)]
        rows = jnp.concatenate([p.reshape(GROUPS * CHUNK, HEAD_DIM) for p in pieces], axis=0)
        sorted_rows = dot_f32(order[...], rows).astype(jnp.bfloat16)
        span = 2 * BLOCK
        for array in range(6):
            piece = sorted_rows[array * span : (array + 1) * span]
            if array < 2:
                for copy in range(8):
                    copies[copy, pl.ds(array * 320 + step * span, span)] = piece
            else:
                own[pl.ds((array - 2) * 320 + step * span, span)] = piece


def unpack(messages):
    order = jnp.asarray(order_matrix(), jnp.bfloat16)
    return pl.pallas_call(
        unpack_kernel,
        out_shape=(
            jax.ShapeDtypeStruct((8, 640, HEAD_DIM), jnp.bfloat16),
            jax.ShapeDtypeStruct((1280, HEAD_DIM), jnp.bfloat16),
        ),
        compiler_params=pltpu.CompilerParams(vmem_limit_bytes=VMEM_LIMIT),
    )(order, messages.reshape(GROUPS, 8, CHUNK, HEAD_DIM))


def block_of(index):
    return jnp.floor((index.astype(jnp.float32) + 0.5) * (1.0 / BLOCK))


def attention_kernel(
    steps, length, planes, own, text_k, text_v, gates, out, keys, values, tk, tv, gate, sems
):
    slot = jnp.minimum(lax.axis_index("z"), GROUP_HEADS - 1)
    columns = pl.ds(pl.multiple_of(slot * HEAD_DIM, HEAD_DIM), HEAD_DIM)
    fetches = [
        pltpu.make_async_copy(text_k.at[:, columns], tk, sems.at[0]),
        pltpu.make_async_copy(text_v.at[:, columns], tv, sems.at[1]),
        pltpu.make_async_copy(gates.at[:, columns], gate, sems.at[2]),
    ]
    for fetch in fetches:
        fetch.start()
    plane = lax.axis_index("x") * 2 + lax.axis_index("yl")
    for place in range(8):
        source = lax.rem(plane + place, 8)
        keys[pl.ds(place * 320, 320)] = planes[source, pl.ds(0, 320)]
        values[pl.ds(place * 320, 320)] = planes[source, pl.ds(320, 320)]
    for fetch in fetches:
        fetch.wait()

    live = lax.broadcasted_iota(jnp.int32, (1, 512), 1) < length[0]
    tile = 160
    finished = []
    for step in range(2):
        gate_row = gate[pl.ds(steps[step], 1), :]
        for first in range(0, 320, tile):
            queries = own[pl.ds(step * 320 + first, tile), :]
            scores = dot_t_f32(queries, keys[...])
            text_scores = jnp.where(live, dot_t_f32(queries, tk[...]), -1e30)
            if step == 1:
                row = block_of(lax.broadcasted_iota(jnp.int32, (tile, 1), 0) + first)
                column = block_of(lax.broadcasted_iota(jnp.int32, (1, 384), 1))
                same = row == column
                near_scores = dot_t_f32(queries, own[pl.ds(640, 384), :])
                near = jnp.where(same, near_scores, scores[:, :384])
                scores = jnp.concatenate([near, scores[:, 384:]], axis=1)
            top = jnp.maximum(
                jnp.max(scores, axis=1, keepdims=True), jnp.max(text_scores, axis=1, keepdims=True)
            )
            raised = jnp.exp2((scores - top) * EXP_SCALE)
            text_raised = jnp.exp2((text_scores - top) * EXP_SCALE)
            total = jnp.sum(raised, axis=1, keepdims=True) + jnp.sum(
                text_raised, axis=1, keepdims=True
            )
            weights = raised.astype(jnp.bfloat16)
            numerator = dot_f32(text_raised.astype(jnp.bfloat16), tv[...])
            if step == 1:
                local = raised[:, :384]
                near_weights = jnp.where(same, local, 0.0).astype(jnp.bfloat16)[:, :320]
                far_weights = jnp.where(same, 0.0, local).astype(jnp.bfloat16)
                numerator += dot_f32(near_weights, own[pl.ds(960, 320), :])
                weights = jnp.concatenate([far_weights, weights[:, 384:]], axis=1)
            numerator += dot_f32(weights, values[...])
            finished.append((gate_row * (numerator / total)).astype(jnp.bfloat16))
    row = lax.broadcasted_iota(jnp.int32, (GROUPS * BACK, BLOCK), 0)
    column = lax.broadcasted_iota(jnp.int32, (GROUPS * BACK, BLOCK), 1)
    place_first = jnp.zeros((GROUPS * BACK, BLOCK), jnp.bool_)
    place_second = jnp.zeros((GROUPS * BACK, BLOCK), jnp.bool_)
    for group in range(GROUPS):
        inside = (column >= group * ROWS) & (column < (group + 1) * ROWS)
        offset = row - group * BACK - column + group * ROWS
        place_first = place_first | (inside & (offset == 0))
        place_second = place_second | (inside & (offset == 8))
    place_first = jnp.where(place_first, 1.0, 0.0).astype(jnp.bfloat16)
    place_second = jnp.where(place_second, 1.0, 0.0).astype(jnp.bfloat16)
    per_tile = tile // BLOCK
    tiles = 320 // tile
    for block in range(8):
        begin = (block % per_tile) * BLOCK
        first_rows = finished[block // per_tile][begin : begin + BLOCK]
        second_rows = finished[tiles + block // per_tile][begin : begin + BLOCK]
        message = dot_f32(place_first, first_rows) + dot_f32(place_second, second_rows)
        out[:, block] = message.astype(jnp.bfloat16).reshape(GROUPS, BACK, HEAD_DIM)


def attention(timesteps, text_length, planes, own, text_keys, text_values, gate_table):
    smem = pl.BlockSpec(memory_space=pltpu.SMEM)
    vmem = pl.BlockSpec(memory_space=pltpu.VMEM)
    hbm = pl.BlockSpec(memory_space=pl.ANY)
    return pl.pallas_call(
        attention_kernel,
        out_shape=jax.ShapeDtypeStruct((GROUPS, 8, BACK, HEAD_DIM), jnp.bfloat16),
        in_specs=[smem, smem, vmem, vmem, hbm, hbm, hbm],
        out_specs=vmem,
        scratch_shapes=[
            pltpu.VMEM((2560, HEAD_DIM), jnp.bfloat16),
            pltpu.VMEM((2560, HEAD_DIM), jnp.bfloat16),
            pltpu.VMEM((512, HEAD_DIM), jnp.bfloat16),
            pltpu.VMEM((512, HEAD_DIM), jnp.bfloat16),
            pltpu.VMEM((35, HEAD_DIM), jnp.float32),
            pltpu.SemaphoreType.DMA((3,)),
        ],
        compiler_params=pltpu.CompilerParams(vmem_limit_bytes=VMEM_LIMIT),
    )(timesteps, text_length, planes, own, text_keys, text_values, gate_table)


def finish_kernel(messages, first, second):
    for group in range(GROUPS):
        for slot in range(GROUP_HEADS):
            head = group * GROUP_HEADS + slot
            columns = pl.ds(head * HEAD_DIM, HEAD_DIM)
            message = messages[group * 8 + slot]
            first[:, columns] = message[0:ROWS]
            second[:, columns] = message[8 : 8 + ROWS]


def finish(messages):
    shape = jax.ShapeDtypeStruct((ROWS, HEADS * HEAD_DIM), jnp.bfloat16)
    return pl.pallas_call(
        finish_kernel,
        out_shape=(shape, shape),
        compiler_params=pltpu.CompilerParams(vmem_limit_bytes=VMEM_LIMIT),
    )(messages)


def body(
    query_first,
    keys_first,
    values_first,
    query_second,
    keys_second,
    values_second,
    text_keys,
    text_values,
    gate_table,
    timesteps,
    text_length,
):
    sent = pack(keys_first, values_first, query_first, query_second, keys_second, values_second)
    arrived = lax.all_to_all(sent, PLANE, 0, 0, tiled=True)
    copies, own = unpack(arrived)
    planes = lax.all_to_all(copies, REPLICAS, 0, 0, tiled=True)
    back = attention(timesteps, text_length, planes, own, text_keys, text_values, gate_table)
    returned = lax.all_to_all(
        back.reshape(64, BACK, HEAD_DIM), PLANE, 0, 0, tiled=True
    )
    return finish(returned)


def solution(mesh):
    fine = Mesh(mesh.devices.reshape(8, 4, 2, 4, 2), AXES)
    rows = P(AXES, None)
    heads = P(None, ("yh", "c"))
    return jax.shard_map(
        body,
        mesh=fine,
        in_specs=(rows,) * 6 + (heads,) * 3 + (P(), P()),
        out_specs=(rows, rows),
        check_vma=False,
    )
```

```python
import jax
import jax.numpy as jnp
import numpy as np
from jax import lax
from jax.experimental import pallas as pl
from jax.experimental.pallas import tpu as pltpu
from jax.sharding import Mesh
from jax.sharding import PartitionSpec as P

HEAD_DIM = 128
HEADS = 40
GROUP_HEADS = 5
PAIR_HEADS = 10
ROWS = 5
PLANE_ROWS = 320
BLOCK_ROWS = 20
PEERS = 64
CHUNK = 32
BACK = 16
TEXT = 512
EXP_SCALE = float(HEAD_DIM ** (-0.5) * np.log2(np.e))

AXES = ("z", "x", "yl", "yh", "c")
PLANE = ("z", "yl", "yh")
ACTIVE = 4 * PAIR_HEADS

NEAR_AT = 4 * 2 * PLANE_ROWS
TEXT_AT = NEAR_AT + 2 * PLANE_ROWS
GATE_AT = TEXT_AT + 2 * TEXT
SHARED = GATE_AT + 16
REST = SHARED - NEAR_AT

VMEM_LIMIT = 48 * 1024 * 1024


def dot_f32(left, right):
    return lax.dot_general(
        left, right, (((1,), (0,)), ((), ())), preferred_element_type=jnp.float32
    )


def dot_t_f32(left, right):
    return lax.dot_general(
        left, right, (((1,), (1,)), ((), ())), preferred_element_type=jnp.float32
    )


def one_hot(condition):
    return jnp.where(condition, 1.0, 0.0).astype(jnp.bfloat16)


def pack_kernel(k1, v1, q1, q2, k2, v2, out, held, sems):
    fetches = [
        pltpu.make_async_copy(array, held.at[index], sems.at[index])
        for index, array in enumerate((k1, v1, q1, q2, k2, v2))
    ]
    for fetch in fetches:
        fetch.start()
    total = None
    for index, fetch in enumerate(fetches):
        row = lax.broadcasted_iota(jnp.int32, (CHUNK, ROWS), 0)
        column = lax.broadcasted_iota(jnp.int32, (CHUNK, ROWS), 1)
        fetch.wait()
        part = dot_f32(one_hot(row == column + index * ROWS), held[index])
        total = part if total is None else total + part
    packed = total.astype(jnp.bfloat16)
    for rank in range(PEERS):
        if rank < ACTIVE:
            head = (rank % 4) * PAIR_HEADS + rank // 4
            out[rank] = packed[:, head * HEAD_DIM : (head + 1) * HEAD_DIM]
        else:
            out[rank] = jnp.zeros((CHUNK, HEAD_DIM), jnp.bfloat16)


def pack(*arrays):
    return pl.pallas_call(
        pack_kernel,
        out_shape=jax.ShapeDtypeStruct((PEERS, CHUNK, HEAD_DIM), jnp.bfloat16),
        in_specs=[pl.BlockSpec(memory_space=pltpu.HBM)] * 6,
        out_specs=pl.BlockSpec(memory_space=pltpu.VMEM),
        scratch_shapes=[
            pltpu.VMEM((6, ROWS, HEADS * HEAD_DIM), jnp.bfloat16),
            pltpu.SemaphoreType.DMA((6,)),
        ],
        compiler_params=pltpu.CompilerParams(vmem_limit_bytes=60 * 1024 * 1024),
    )(*arrays)


def head_slot():
    return lax.axis_index("z") * 2 + lax.axis_index("yl")


def unpack_kernel(steps, messages, text_k, text_v, gates, copies, queries, rest, gate, sems):
    slot = lax.rem(head_slot(), GROUP_HEADS)
    columns = pl.ds(pl.multiple_of(slot * HEAD_DIM, HEAD_DIM), HEAD_DIM)
    text_at = TEXT_AT - NEAR_AT
    fetches = [
        pltpu.make_async_copy(text_k.at[:, columns], rest.at[pl.ds(text_at, TEXT)], sems.at[0]),
        pltpu.make_async_copy(
            text_v.at[:, columns], rest.at[pl.ds(text_at + TEXT, TEXT)], sems.at[1]
        ),
        pltpu.make_async_copy(gates.at[:, columns], gate, sems.at[2]),
    ]
    for fetch in fetches:
        fetch.start()
    source = lax.broadcasted_iota(jnp.int32, (1, 512), 1)
    message, entry = source // CHUNK, source % CHUNK
    target = entry + ((entry * 13) // 64) * 75 + message * ROWS
    order = one_hot(lax.broadcasted_iota(jnp.int32, (480, 512), 0) == target)
    for step in range(4):
        rows = messages[pl.ds(step * 16, 16)].reshape(512, HEAD_DIM)
        ordered = dot_f32(order, rows).astype(jnp.bfloat16)
        for array in range(6):
            piece = ordered[array * 80 : (array + 1) * 80]
            place = pl.ds((array % 2) * PLANE_ROWS + step * 80, 80)
            if array < 2:
                for copy in range(4):
                    copies[copy, place] = piece
            elif array < 4:
                queries[place] = piece
            else:
                rest[place] = piece
    for fetch in fetches:
        fetch.wait()
    row = lax.broadcasted_iota(jnp.int32, (16, HEAD_DIM), 0)
    parts = jnp.zeros((16, HEAD_DIM), jnp.float32)
    for step in range(2):
        left = gate[pl.ds(steps[step], 1), :]
        for index in range(3):
            part = left.astype(jnp.bfloat16).astype(jnp.float32)
            parts = jnp.where(row == step * 3 + index, part, parts)
            left = left - part
    rest[pl.ds(GATE_AT - NEAR_AT, 16)] = parts.astype(jnp.bfloat16)


def unpack(timesteps, messages, text_keys, text_values, gate_table):
    vmem = pl.BlockSpec(memory_space=pltpu.VMEM)
    hbm = pl.BlockSpec(memory_space=pl.ANY)
    return pl.pallas_call(
        unpack_kernel,
        out_shape=(
            jax.ShapeDtypeStruct((4, 2 * PLANE_ROWS, HEAD_DIM), jnp.bfloat16),
            jax.ShapeDtypeStruct((2 * PLANE_ROWS, HEAD_DIM), jnp.bfloat16),
            jax.ShapeDtypeStruct((REST, HEAD_DIM), jnp.bfloat16),
        ),
        in_specs=[pl.BlockSpec(memory_space=pltpu.SMEM), vmem, hbm, hbm, hbm],
        out_specs=(vmem, vmem, vmem),
        scratch_shapes=[
            pltpu.VMEM((35, HEAD_DIM), jnp.float32),
            pltpu.SemaphoreType.DMA((3,)),
        ],
        compiler_params=pltpu.CompilerParams(vmem_limit_bytes=VMEM_LIMIT),
    )(timesteps, messages, text_keys, text_values, gate_table)


def join_kernel(planes, rest, out):
    out[pl.ds(0, NEAR_AT)] = planes[...].reshape(NEAR_AT, HEAD_DIM)
    out[pl.ds(NEAR_AT, REST)] = rest[...]


def join(planes, rest):
    return pl.pallas_call(
        join_kernel,
        out_shape=jax.ShapeDtypeStruct((SHARED, HEAD_DIM), jnp.bfloat16),
        compiler_params=pltpu.CompilerParams(vmem_limit_bytes=VMEM_LIMIT),
    )(planes, rest)


def block_of(index):
    return jnp.floor((index.astype(jnp.float32) + 0.5) * (1.0 / BLOCK_ROWS))


def attention_kernel(length, queries, mine, theirs, out, keys, values, text):
    own = lax.axis_index("x")
    for place in range(4):
        begin = pl.multiple_of(lax.rem(own + place, 4) * (2 * PLANE_ROWS), 2 * PLANE_ROWS)
        for side, shared in enumerate((mine, theirs)):
            target = pl.ds((place * 2 + side) * PLANE_ROWS, PLANE_ROWS)
            keys[target] = shared[pl.ds(begin, PLANE_ROWS)]
            values[target] = shared[pl.ds(begin + PLANE_ROWS, PLANE_ROWS)]
    here = head_slot() // GROUP_HEADS == lax.axis_index("c")

    @pl.when(here)
    def _():
        text[...] = mine[pl.ds(TEXT_AT, SHARED - TEXT_AT)]

    @pl.when(jnp.logical_not(here))
    def _():
        text[...] = theirs[pl.ds(TEXT_AT, SHARED - TEXT_AT)]

    near_keys, near_values = [
        jnp.concatenate([shared[pl.ds(begin, PLANE_ROWS)] for shared in (mine, theirs)], axis=0)
        for begin in (NEAR_AT, NEAR_AT + PLANE_ROWS)
    ]
    near = 2 * PLANE_ROWS
    parts = text[pl.ds(2 * TEXT, 16)].astype(jnp.float32)
    live = lax.broadcasted_iota(jnp.int32, (1, TEXT), 1) < length[0]
    column = lax.broadcasted_iota(jnp.int32, (1, near), 1)
    column_block = block_of(jnp.where(column < PLANE_ROWS, column, column - PLANE_ROWS))
    tile = 160
    finished = []
    for step in range(2):
        gate_row = parts[3 * step : 3 * step + 1] + parts[3 * step + 1 : 3 * step + 2]
        gate_row = gate_row + parts[3 * step + 2 : 3 * step + 3]
        for first in range(0, PLANE_ROWS, tile):
            rows = queries[pl.ds(step * PLANE_ROWS + first, tile), :]
            scores = dot_t_f32(rows, keys[...])
            text_scores = jnp.where(live, dot_t_f32(rows, text[pl.ds(0, TEXT)]), -1e30)
            if step == 1:
                row = block_of(lax.broadcasted_iota(jnp.int32, (tile, 1), 0) + first)
                same = row == column_block
                near_scores = jnp.where(same, dot_t_f32(rows, near_keys), scores[:, :near])
                scores = jnp.concatenate([near_scores, scores[:, near:]], axis=1)
            top = jnp.maximum(
                jnp.max(scores, axis=1, keepdims=True), jnp.max(text_scores, axis=1, keepdims=True)
            )
            raised = jnp.exp2((scores - top) * EXP_SCALE)
            text_raised = jnp.exp2((text_scores - top) * EXP_SCALE)
            total = jnp.sum(raised, axis=1, keepdims=True) + jnp.sum(
                text_raised, axis=1, keepdims=True
            )
            weights = raised.astype(jnp.bfloat16)
            numerator = dot_f32(text_raised.astype(jnp.bfloat16), text[pl.ds(TEXT, TEXT)])
            if step == 1:
                local = raised[:, :near]
                numerator += dot_f32(jnp.where(same, local, 0.0).astype(jnp.bfloat16), near_values)
                far = jnp.where(same, 0.0, local).astype(jnp.bfloat16)
                weights = jnp.concatenate([far, weights[:, near:]], axis=1)
            numerator += dot_f32(weights, values[...])
            finished.append((gate_row * (numerator / total)).astype(jnp.bfloat16))
    row = lax.broadcasted_iota(jnp.int32, (16 * BACK, 80), 0)
    column = lax.broadcasted_iota(jnp.int32, (16 * BACK, 80), 1)
    entry = row % BACK
    begin = (row // BACK) * ROWS
    place_first = one_hot((column == begin + entry) & (entry < ROWS))
    place_second = one_hot((column == begin + entry - 8) & (entry >= 8) & (entry < 8 + ROWS))
    for part in range(4):
        index, begin = part // 2, (part % 2) * 80
        message = dot_f32(place_first, finished[index][begin : begin + 80])
        message += dot_f32(place_second, finished[2 + index][begin : begin + 80])
        out[pl.ds(part * 16, 16)] = message.astype(jnp.bfloat16).reshape(16, BACK, HEAD_DIM)


def attention(text_length, queries, mine, theirs):
    vmem = pl.BlockSpec(memory_space=pltpu.VMEM)
    return pl.pallas_call(
        attention_kernel,
        out_shape=jax.ShapeDtypeStruct((PEERS, BACK, HEAD_DIM), jnp.bfloat16),
        in_specs=[pl.BlockSpec(memory_space=pltpu.SMEM), vmem, vmem, vmem],
        out_specs=vmem,
        scratch_shapes=[
            pltpu.VMEM((8 * PLANE_ROWS, HEAD_DIM), jnp.bfloat16),
            pltpu.VMEM((8 * PLANE_ROWS, HEAD_DIM), jnp.bfloat16),
            pltpu.VMEM((SHARED - TEXT_AT, HEAD_DIM), jnp.bfloat16),
        ],
        compiler_params=pltpu.CompilerParams(vmem_limit_bytes=VMEM_LIMIT),
    )(text_length, queries, mine, theirs)


def finish_kernel(messages, first, second):
    for rank in range(ACTIVE):
        head = (rank % 4) * PAIR_HEADS + rank // 4
        columns = pl.ds(head * HEAD_DIM, HEAD_DIM)
        message = messages[rank]
        first[:, columns] = message[0:ROWS]
        second[:, columns] = message[8 : 8 + ROWS]


def finish(messages):
    shape = jax.ShapeDtypeStruct((ROWS, HEADS * HEAD_DIM), jnp.bfloat16)
    return pl.pallas_call(
        finish_kernel,
        out_shape=(shape, shape),
        compiler_params=pltpu.CompilerParams(vmem_limit_bytes=VMEM_LIMIT),
    )(messages)


def body(
    query_first,
    keys_first,
    values_first,
    query_second,
    keys_second,
    values_second,
    text_keys,
    text_values,
    gate_table,
    timesteps,
    text_length,
):
    sent = pack(keys_first, values_first, query_first, query_second, keys_second, values_second)
    arrived = lax.all_to_all(sent, PLANE, 0, 0, tiled=True)
    copies, queries, rest = unpack(timesteps, arrived, text_keys, text_values, gate_table)
    planes = lax.all_to_all(copies, "x", 0, 0, tiled=True)
    mine = join(planes, rest)
    theirs = lax.ppermute(mine, "c", [(0, 1), (1, 0)])
    back = attention(text_length, queries, mine, theirs)
    returned = lax.all_to_all(back, PLANE, 0, 0, tiled=True)
    return finish(returned)


def solution(mesh):
    fine = Mesh(mesh.devices.reshape(8, 4, 2, 4, 2), AXES)
    rows = P(AXES, None)
    heads = P(None, ("yh", "c"))
    return jax.shard_map(
        body,
        mesh=fine,
        in_specs=(rows,) * 6 + (heads,) * 3 + (P(), P()),
        out_specs=(rows, rows),
        check_vma=False,
    )
```

```python
import jax
import jax.numpy as jnp
import numpy as np
from jax import lax
from jax.experimental import pallas as pl
from jax.experimental.pallas import tpu as pltpu
from jax.sharding import Mesh
from jax.sharding import PartitionSpec as P

HEAD_DIM = 128
HEADS = 40
GROUP_HEADS = 5
PAIR_HEADS = 10
ROWS = 5
PLANE_ROWS = 320
BLOCK_ROWS = 20
PEERS = 64
CHUNK = 32
BACK = 16
TEXT = 512
EXP_SCALE = float(HEAD_DIM ** (-0.5) * np.log2(np.e))

AXES = ("z", "x", "yl", "yh", "c")
PLANE = ("z", "yl", "yh")
ACTIVE = 4 * PAIR_HEADS

HALF = 4 * PLANE_ROWS
NEAR_AT = 2 * HALF
TEXT_AT = NEAR_AT + 2 * PLANE_ROWS
GATE_AT = TEXT_AT + 2 * TEXT
SHARED = GATE_AT + 16
REST = SHARED - NEAR_AT

VMEM_LIMIT = 48 * 1024 * 1024


def dot_f32(left, right):
    return lax.dot_general(
        left, right, (((1,), (0,)), ((), ())), preferred_element_type=jnp.float32
    )


def dot_t_f32(left, right):
    return lax.dot_general(
        left, right, (((1,), (1,)), ((), ())), preferred_element_type=jnp.float32
    )


def in_hbm(array):
    return pltpu.with_memory_space_constraint(array, pltpu.HBM)


def one_hot(condition):
    return jnp.where(condition, 1.0, 0.0).astype(jnp.bfloat16)


def pack_kernel(k1, v1, q1, q2, k2, v2, out, held, sems):
    fetches = [
        pltpu.make_async_copy(array, held.at[index], sems.at[index])
        for index, array in enumerate((k1, v1, q1, q2, k2, v2))
    ]
    for fetch in fetches:
        fetch.start()
    total = None
    for index, fetch in enumerate(fetches):
        row = lax.broadcasted_iota(jnp.int32, (CHUNK, ROWS), 0)
        column = lax.broadcasted_iota(jnp.int32, (CHUNK, ROWS), 1)
        fetch.wait()
        part = dot_f32(one_hot(row == column + index * ROWS), held[index])
        total = part if total is None else total + part
    packed = total.astype(jnp.bfloat16)
    for rank in range(PEERS):
        if rank < ACTIVE:
            head = (rank % 4) * PAIR_HEADS + rank // 4
            out[rank] = packed[:, head * HEAD_DIM : (head + 1) * HEAD_DIM]
        else:
            out[rank] = jnp.zeros((CHUNK, HEAD_DIM), jnp.bfloat16)


def pack(*arrays):
    return pl.pallas_call(
        pack_kernel,
        out_shape=jax.ShapeDtypeStruct((PEERS, CHUNK, HEAD_DIM), jnp.bfloat16),
        in_specs=[pl.BlockSpec(memory_space=pltpu.HBM)] * 6,
        out_specs=pl.BlockSpec(memory_space=pltpu.VMEM),
        scratch_shapes=[
            pltpu.VMEM((6, ROWS, HEADS * HEAD_DIM), jnp.bfloat16),
            pltpu.SemaphoreType.DMA((6,)),
        ],
        compiler_params=pltpu.CompilerParams(vmem_limit_bytes=VMEM_LIMIT),
    )(*[in_hbm(array) for array in arrays])


def head_slot():
    return lax.axis_index("z") * 2 + lax.axis_index("yl")


def unpack_kernel(steps, messages, text_k, text_v, gates, copies, queries, rest, gate, sems):
    slot = lax.rem(head_slot(), GROUP_HEADS)
    columns = pl.ds(pl.multiple_of(slot * HEAD_DIM, HEAD_DIM), HEAD_DIM)
    text_at = TEXT_AT - NEAR_AT
    fetches = [
        pltpu.make_async_copy(text_k.at[:, columns], rest.at[pl.ds(text_at, TEXT)], sems.at[0]),
        pltpu.make_async_copy(
            text_v.at[:, columns], rest.at[pl.ds(text_at + TEXT, TEXT)], sems.at[1]
        ),
        pltpu.make_async_copy(gates.at[:, columns], gate, sems.at[2]),
    ]
    for fetch in fetches:
        fetch.start()
    source = lax.broadcasted_iota(jnp.int32, (1, 256), 1)
    message, entry = source // CHUNK, source % CHUNK
    target = entry + ((entry * 13) // 64) * 35 + message * ROWS
    order = one_hot(lax.broadcasted_iota(jnp.int32, (240, 256), 0) == target)
    for step in range(8):
        rows = messages[pl.ds(step * 8, 8)].reshape(256, HEAD_DIM)
        ordered = dot_f32(order, rows).astype(jnp.bfloat16)
        for array in range(6):
            piece = ordered[array * 40 : (array + 1) * 40]
            place = pl.ds((array % 2) * PLANE_ROWS + step * 40, 40)
            if array < 2:
                for copy in range(4):
                    copies[copy, place] = piece
            elif array < 4:
                queries[place] = piece
            else:
                rest[place] = piece
    for fetch in fetches:
        fetch.wait()
    row = lax.broadcasted_iota(jnp.int32, (16, HEAD_DIM), 0)
    parts = jnp.zeros((16, HEAD_DIM), jnp.float32)
    for step in range(2):
        left = gate[pl.ds(steps[step], 1), :]
        for index in range(3):
            part = left.astype(jnp.bfloat16).astype(jnp.float32)
            parts = jnp.where(row == step * 3 + index, part, parts)
            left = left - part
    rest[pl.ds(GATE_AT - NEAR_AT, 16)] = parts.astype(jnp.bfloat16)


def unpack(timesteps, messages, text_keys, text_values, gate_table):
    vmem = pl.BlockSpec(memory_space=pltpu.VMEM)
    hbm = pl.BlockSpec(memory_space=pltpu.HBM)
    return pl.pallas_call(
        unpack_kernel,
        out_shape=(
            jax.ShapeDtypeStruct((4, 2 * PLANE_ROWS, HEAD_DIM), jnp.bfloat16),
            jax.ShapeDtypeStruct((2 * PLANE_ROWS, HEAD_DIM), jnp.bfloat16),
            jax.ShapeDtypeStruct((REST, HEAD_DIM), jnp.bfloat16),
        ),
        in_specs=[pl.BlockSpec(memory_space=pltpu.SMEM), vmem, hbm, hbm, hbm],
        out_specs=(vmem, vmem, vmem),
        scratch_shapes=[
            pltpu.VMEM((35, HEAD_DIM), jnp.float32),
            pltpu.SemaphoreType.DMA((3,)),
        ],
        compiler_params=pltpu.CompilerParams(vmem_limit_bytes=VMEM_LIMIT),
    )(timesteps, messages, in_hbm(text_keys), in_hbm(text_values), in_hbm(gate_table))


def join_kernel(planes, rest, out):
    own = lax.axis_index("x")
    for place in range(4):
        source = lax.rem(own + place, 4)
        for part in range(2):
            out[pl.ds(part * HALF + place * PLANE_ROWS, PLANE_ROWS)] = planes[
                source, pl.ds(part * PLANE_ROWS, PLANE_ROWS)
            ]
    out[pl.ds(NEAR_AT, REST)] = rest[...]


def join(planes, rest):
    return pl.pallas_call(
        join_kernel,
        out_shape=jax.ShapeDtypeStruct((SHARED, HEAD_DIM), jnp.bfloat16),
        compiler_params=pltpu.CompilerParams(vmem_limit_bytes=VMEM_LIMIT),
    )(planes, rest)


TILE = 160
TILES = 2 * PLANE_ROWS // TILE
NEAR = 384
CUTS = ((0, 512), (512, 1024), (1024, HALF))


def block_of(index):
    return jnp.floor((index.astype(jnp.float32) + 0.5) * (1.0 / BLOCK_ROWS))


def beside_ones(target, rows):
    target[:, :HEAD_DIM] = rows
    target[:, HEAD_DIM:] = jnp.ones_like(rows)


def same_block(tile):
    row = lax.broadcasted_iota(jnp.int32, (TILE, 1), 0) + (tile * TILE) % PLANE_ROWS
    column = lax.broadcasted_iota(jnp.int32, (1, NEAR), 1)
    return block_of(row) == block_of(column)


def tile_rows(tile):
    return pl.ds(tile * TILE, TILE)


def half_scores(queries, keys, tile, cut):
    rows = queries[tile_rows(tile)]
    scores = dot_t_f32(rows, keys[pl.ds(cut[0], cut[1] - cut[0])])
    if tile * TILE >= PLANE_ROWS and cut[0] == 0:
        near = dot_t_f32(rows, keys[pl.ds(NEAR_AT, NEAR)])
        near = jnp.where(same_block(tile), near, scores[:, :NEAR])
        scores = jnp.concatenate([near, scores[:, NEAR:]], axis=1)
    return scores


def half_sums(weights, values, near_values, tile, cut):
    part = values[pl.ds(cut[0], cut[1] - cut[0])]
    if tile * TILE >= PLANE_ROWS and cut[0] == 0:
        same = same_block(tile)
        local = weights[:, :NEAR]
        blank = jnp.zeros_like(local)
        far = jnp.concatenate([jnp.where(same, blank, local), weights[:, NEAR:]], axis=1)
        return dot_f32(far, part) + dot_f32(jnp.where(same, local, blank), near_values[...])
    return dot_f32(weights, part)


def lane_max(scores, former):
    for begin in range(0, scores.shape[1], HEAD_DIM):
        piece = scores[:, begin : begin + HEAD_DIM]
        former = piece if former is None else jnp.maximum(former, piece)
    return former


def weigh(scores, top):
    return jnp.exp2((scores - top) * EXP_SCALE).astype(jnp.bfloat16)


def run_tiles(score_parts, sum_parts, start_top, finish_tile):
    former = None
    for tile in range(TILES + 1):
        scores, lanes, sums = [], None, None
        for index in range(len(score_parts)):
            if tile < TILES:
                part = score_parts[index](tile)
                lanes = lane_max(part, lanes)
                scores.append(part)
            if former is not None:
                part = sum_parts[index](weigh(former[0][index], former[1]), tile - 1)
                sums = part if sums is None else sums + part
        if former is not None:
            finish_tile(tile - 1, former[1], sums)
        if tile < TILES:
            top = jnp.max(lanes, axis=1, keepdims=True)
            former = (scores, start_top(tile, top))


def first_kernel(queries, mine, sums, tops, values, near_values):
    beside_ones(values, mine[pl.ds(HALF, HALF)])
    beside_ones(near_values, mine[pl.ds(NEAR_AT + PLANE_ROWS, NEAR)])

    def finish_tile(tile, top, total):
        sums[tile_rows(tile)] = total
        tops[tile_rows(tile)] = jnp.broadcast_to(top, (TILE, HEAD_DIM))

    run_tiles(
        [lambda tile, cut=cut: half_scores(queries, mine, tile, cut) for cut in CUTS],
        [
            lambda weights, tile, cut=cut: half_sums(weights, values, near_values, tile, cut)
            for cut in CUTS
        ],
        lambda tile, top: top,
        finish_tile,
    )


def second_kernel(
    length, queries, mine, theirs, sums, tops, out, values, near_values, text, text_values, done
):
    here = head_slot() // GROUP_HEADS == lax.axis_index("c")

    @pl.when(here)
    def _():
        text[...] = mine[pl.ds(TEXT_AT, SHARED - TEXT_AT)]

    @pl.when(jnp.logical_not(here))
    def _():
        text[...] = theirs[pl.ds(TEXT_AT, SHARED - TEXT_AT)]

    beside_ones(values, theirs[pl.ds(HALF, HALF)])
    beside_ones(near_values, theirs[pl.ds(NEAR_AT + PLANE_ROWS, NEAR)])
    beside_ones(text_values, text[pl.ds(TEXT, TEXT)])
    parts = text[pl.ds(2 * TEXT, 16)].astype(jnp.float32)
    live = lax.broadcasted_iota(jnp.int32, (1, TEXT), 1) < length[0]

    def text_scores(tile):
        scores = dot_t_f32(queries[tile_rows(tile)], text[pl.ds(0, TEXT)])
        return jnp.where(live, scores, -1e30)

    def start_top(tile, top):
        return jnp.maximum(tops[tile_rows(tile), 0:1], top)

    def finish_tile(tile, top, total):
        former = jnp.exp2((tops[tile_rows(tile), 0:1] - top) * EXP_SCALE)
        total = total + sums[tile_rows(tile)] * former
        step = tile * TILE // PLANE_ROWS
        gate = parts[3 * step : 3 * step + 1] + parts[3 * step + 1 : 3 * step + 2]
        gate = gate + parts[3 * step + 2 : 3 * step + 3]
        attended = total[:, :HEAD_DIM] / total[:, HEAD_DIM:]
        done[tile_rows(tile)] = (gate * attended).astype(jnp.bfloat16)

    run_tiles(
        [lambda tile, cut=cut: half_scores(queries, theirs, tile, cut) for cut in CUTS]
        + [text_scores],
        [
            lambda weights, tile, cut=cut: half_sums(weights, values, near_values, tile, cut)
            for cut in CUTS
        ]
        + [lambda weights, tile: dot_f32(weights, text_values[...])],
        start_top,
        finish_tile,
    )
    row = lax.broadcasted_iota(jnp.int32, (16 * BACK, 80), 0)
    column = lax.broadcasted_iota(jnp.int32, (16 * BACK, 80), 1)
    entry = row % BACK
    begin = (row // BACK) * ROWS
    place_first = one_hot((column == begin + entry) & (entry < ROWS))
    place_second = one_hot((column == begin + entry - 8) & (entry >= 8) & (entry < 8 + ROWS))
    for part in range(4):
        message = dot_f32(place_first, done[pl.ds(part * 80, 80)])
        message += dot_f32(place_second, done[pl.ds(PLANE_ROWS + part * 80, 80)])
        out[pl.ds(part * 16, 16)] = message.astype(jnp.bfloat16).reshape(16, BACK, HEAD_DIM)


def first_pass(queries, mine):
    vmem = pl.BlockSpec(memory_space=pltpu.VMEM)
    return pl.pallas_call(
        first_kernel,
        out_shape=(
            jax.ShapeDtypeStruct((2 * PLANE_ROWS, 2 * HEAD_DIM), jnp.float32),
            jax.ShapeDtypeStruct((2 * PLANE_ROWS, HEAD_DIM), jnp.float32),
        ),
        in_specs=[vmem, vmem],
        out_specs=(vmem, vmem),
        scratch_shapes=[
            pltpu.VMEM((HALF, 2 * HEAD_DIM), jnp.bfloat16),
            pltpu.VMEM((NEAR, 2 * HEAD_DIM), jnp.bfloat16),
        ],
        cost_estimate=pl.CostEstimate(
            flops=4 * 640 * 1600 * HEAD_DIM, bytes_accessed=2 * SHARED * HEAD_DIM, transcendentals=640 * HALF
        ),
        compiler_params=pltpu.CompilerParams(vmem_limit_bytes=VMEM_LIMIT),
    )(queries, mine)


def second_pass(text_length, queries, mine, theirs, sums, tops):
    vmem = pl.BlockSpec(memory_space=pltpu.VMEM)
    return pl.pallas_call(
        second_kernel,
        out_shape=jax.ShapeDtypeStruct((PEERS, BACK, HEAD_DIM), jnp.bfloat16),
        in_specs=[pl.BlockSpec(memory_space=pltpu.SMEM)] + [vmem] * 5,
        out_specs=vmem,
        scratch_shapes=[
            pltpu.VMEM((HALF, 2 * HEAD_DIM), jnp.bfloat16),
            pltpu.VMEM((NEAR, 2 * HEAD_DIM), jnp.bfloat16),
            pltpu.VMEM((SHARED - TEXT_AT, HEAD_DIM), jnp.bfloat16),
            pltpu.VMEM((TEXT, 2 * HEAD_DIM), jnp.bfloat16),
            pltpu.VMEM((2 * PLANE_ROWS, HEAD_DIM), jnp.bfloat16),
        ],
        compiler_params=pltpu.CompilerParams(vmem_limit_bytes=VMEM_LIMIT),
    )(text_length, queries, mine, theirs, sums, tops)


def finish_kernel(messages, first, second):
    for rank in range(ACTIVE):
        head = (rank % 4) * PAIR_HEADS + rank // 4
        columns = pl.ds(head * HEAD_DIM, HEAD_DIM)
        message = messages[rank]
        first[:, columns] = message[0:ROWS]
        second[:, columns] = message[8 : 8 + ROWS]


def finish(messages):
    shape = jax.ShapeDtypeStruct((ROWS, HEADS * HEAD_DIM), jnp.bfloat16)
    return pl.pallas_call(
        finish_kernel,
        out_shape=(shape, shape),
        compiler_params=pltpu.CompilerParams(vmem_limit_bytes=VMEM_LIMIT),
    )(messages)


def body(
    query_first,
    keys_first,
    values_first,
    query_second,
    keys_second,
    values_second,
    text_keys,
    text_values,
    gate_table,
    timesteps,
    text_length,
):
    sent = pack(keys_first, values_first, query_first, query_second, keys_second, values_second)
    arrived = lax.all_to_all(sent, PLANE, 0, 0, tiled=True)
    copies, queries, rest = unpack(timesteps, arrived, text_keys, text_values, gate_table)
    planes = lax.all_to_all(copies, "x", 0, 0, tiled=True)
    mine = join(planes, rest)
    theirs = lax.ppermute(mine, "c", [(0, 1), (1, 0)])
    sums, tops = first_pass(queries, mine)
    back = second_pass(text_length, queries, mine, theirs, sums, tops)
    returned = lax.all_to_all(back, PLANE, 0, 0, tiled=True)
    return finish(returned)


def solution(mesh):
    fine = Mesh(mesh.devices.reshape(8, 4, 2, 4, 2), AXES)
    rows = P(AXES, None)
    heads = P(None, ("yh", "c"))
    return jax.shard_map(
        body,
        mesh=fine,
        in_specs=(rows,) * 6 + (heads,) * 3 + (P(), P()),
        out_specs=(rows, rows),
        check_vma=False,
    )
```

```python
import jax
import jax.numpy as jnp
import numpy as np
from jax import lax
from jax.experimental import pallas as pl
from jax.experimental.pallas import tpu as pltpu
from jax.sharding import Mesh
from jax.sharding import PartitionSpec as P

HEAD_DIM = 128
HEADS = 40
GROUP_HEADS = 5
PAIR_HEADS = 10
ROWS = 5
PLANE_ROWS = 320
BLOCK_ROWS = 20
PEERS = 64
CHUNK = 32
BACK = 16
TEXT = 512
EXP_SCALE = float(HEAD_DIM ** (-0.5) * np.log2(np.e))

AXES = ("z", "x", "yl", "yh", "c")
PLANE = ("z", "yl", "yh")
ACTIVE = 4 * PAIR_HEADS

HALF = 4 * PLANE_ROWS
NEAR_AT = 2 * HALF
TEXT_AT = NEAR_AT + 2 * PLANE_ROWS
GATE_AT = TEXT_AT + 2 * TEXT
SHARED = GATE_AT + 16
EXTRA = SHARED - TEXT_AT

VMEM_LIMIT = 48 * 1024 * 1024


def dot_f32(left, right):
    return lax.dot_general(
        left, right, (((1,), (0,)), ((), ())), preferred_element_type=jnp.float32
    )


def dot_t_f32(left, right):
    return lax.dot_general(
        left, right, (((1,), (1,)), ((), ())), preferred_element_type=jnp.float32
    )


def head_slot():
    return lax.axis_index("z") * 2 + lax.axis_index("yl")


def in_hbm(array):
    return pltpu.with_memory_space_constraint(array, pltpu.HBM)


def one_hot(condition):
    return jnp.where(condition, 1.0, 0.0).astype(jnp.bfloat16)


def pack_kernel(
    k1, v1, q1, q2, k2, v2, text_k, text_v, gates, steps, out, extra, held, gate, step_ids, sems
):
    slot = lax.rem(head_slot(), GROUP_HEADS)
    columns = pl.ds(pl.multiple_of(slot * HEAD_DIM, HEAD_DIM), HEAD_DIM)
    targets = [(array, held.at[index]) for index, array in enumerate((k1, v1, q1, q2, k2, v2))]
    targets += [
        (steps, step_ids),
        (gates.at[:, columns], gate),
        (text_k.at[:, columns], extra.at[pl.ds(0, TEXT)]),
        (text_v.at[:, columns], extra.at[pl.ds(TEXT, TEXT)]),
    ]
    fetches = [
        pltpu.make_async_copy(source, target, sems.at[index])
        for index, (source, target) in enumerate(targets)
    ]
    for fetch in fetches:
        fetch.start()
    total = None
    for index in range(6):
        row = lax.broadcasted_iota(jnp.int32, (CHUNK, ROWS), 0)
        column = lax.broadcasted_iota(jnp.int32, (CHUNK, ROWS), 1)
        fetches[index].wait()
        part = dot_f32(one_hot(row == column + index * ROWS), held[index])
        total = part if total is None else total + part
    packed = total.astype(jnp.bfloat16)
    for rank in range(PEERS):
        if rank < ACTIVE:
            head = (rank % 4) * PAIR_HEADS + rank // 4
            out[rank] = packed[:, head * HEAD_DIM : (head + 1) * HEAD_DIM]
        else:
            out[rank] = jnp.zeros((CHUNK, HEAD_DIM), jnp.bfloat16)
    for fetch in fetches[6:]:
        fetch.wait()
    row = lax.broadcasted_iota(jnp.int32, (16, HEAD_DIM), 0)
    parts = jnp.zeros((16, HEAD_DIM), jnp.float32)
    for step in range(2):
        left = gate[pl.ds(step_ids[step], 1), :]
        for index in range(3):
            part = left.astype(jnp.bfloat16).astype(jnp.float32)
            parts = jnp.where(row == step * 3 + index, part, parts)
            left = left - part
    extra[pl.ds(2 * TEXT, 16)] = parts.astype(jnp.bfloat16)


def pack(*arrays):
    vmem = pl.BlockSpec(memory_space=pltpu.VMEM)
    return pl.pallas_call(
        pack_kernel,
        out_shape=(
            jax.ShapeDtypeStruct((PEERS, CHUNK, HEAD_DIM), jnp.bfloat16),
            jax.ShapeDtypeStruct((EXTRA, HEAD_DIM), jnp.bfloat16),
        ),
        in_specs=[pl.BlockSpec(memory_space=pltpu.HBM)] * 10,
        out_specs=(vmem, vmem),
        scratch_shapes=[
            pltpu.VMEM((6, ROWS, HEADS * HEAD_DIM), jnp.bfloat16),
            pltpu.VMEM((35, HEAD_DIM), jnp.float32),
            pltpu.SMEM((2,), jnp.int32),
            pltpu.SemaphoreType.DMA((10,)),
        ],
        compiler_params=pltpu.CompilerParams(vmem_limit_bytes=VMEM_LIMIT),
    )(*[in_hbm(array) for array in arrays])


def unpack_kernel(messages, copies, queries, near):
    source = lax.broadcasted_iota(jnp.int32, (1, 256), 1)
    message, entry = source // CHUNK, source % CHUNK
    target = entry + ((entry * 13) // 64) * 35 + message * ROWS
    order = one_hot(lax.broadcasted_iota(jnp.int32, (240, 256), 0) == target)
    for step in range(8):
        rows = messages[pl.ds(step * 8, 8)].reshape(256, HEAD_DIM)
        ordered = dot_f32(order, rows).astype(jnp.bfloat16)
        for array in range(6):
            piece = ordered[array * 40 : (array + 1) * 40]
            place = pl.ds((array % 2) * PLANE_ROWS + step * 40, 40)
            if array < 2:
                for copy in range(4):
                    copies[copy, place] = piece
            elif array < 4:
                queries[place] = piece
            else:
                near[place] = piece


def unpack(messages):
    rows = jax.ShapeDtypeStruct((2 * PLANE_ROWS, HEAD_DIM), jnp.bfloat16)
    return pl.pallas_call(
        unpack_kernel,
        out_shape=(
            jax.ShapeDtypeStruct((4, 2 * PLANE_ROWS, HEAD_DIM), jnp.bfloat16),
            rows,
            rows,
        ),
        compiler_params=pltpu.CompilerParams(vmem_limit_bytes=VMEM_LIMIT),
    )(messages)


def join_kernel(planes, near, extra, out):
    own = lax.axis_index("x")
    for place in range(4):
        source = lax.rem(own + place, 4)
        for part in range(2):
            out[pl.ds(part * HALF + place * PLANE_ROWS, PLANE_ROWS)] = planes[
                source, pl.ds(part * PLANE_ROWS, PLANE_ROWS)
            ]
    out[pl.ds(NEAR_AT, 2 * PLANE_ROWS)] = near[...]
    out[pl.ds(TEXT_AT, EXTRA)] = extra[...]


def join(planes, near, extra):
    return pl.pallas_call(
        join_kernel,
        out_shape=jax.ShapeDtypeStruct((SHARED, HEAD_DIM), jnp.bfloat16),
        compiler_params=pltpu.CompilerParams(vmem_limit_bytes=VMEM_LIMIT),
    )(planes, near, extra)


TILE = 160
TILES = 2 * PLANE_ROWS // TILE
NEAR = 384
CUTS = ((0, 512), (512, 1024), (1024, HALF))


def block_of(index):
    return jnp.floor((index.astype(jnp.float32) + 0.5) * (1.0 / BLOCK_ROWS))


def beside_ones(target, rows):
    target[:, :HEAD_DIM] = rows
    target[:, HEAD_DIM:] = jnp.ones_like(rows)


def same_block(tile):
    row = lax.broadcasted_iota(jnp.int32, (TILE, 1), 0) + (tile * TILE) % PLANE_ROWS
    column = lax.broadcasted_iota(jnp.int32, (1, NEAR), 1)
    return block_of(row) == block_of(column)


def tile_rows(tile):
    return pl.ds(tile * TILE, TILE)


def half_scores(queries, keys, tile, cut):
    rows = queries[tile_rows(tile)]
    scores = dot_t_f32(rows, keys[pl.ds(cut[0], cut[1] - cut[0])])
    if tile * TILE >= PLANE_ROWS and cut[0] == 0:
        near = dot_t_f32(rows, keys[pl.ds(NEAR_AT, NEAR)])
        near = jnp.where(same_block(tile), near, scores[:, :NEAR])
        scores = jnp.concatenate([near, scores[:, NEAR:]], axis=1)
    return scores


def half_sums(weights, values, near_values, tile, cut):
    part = values[pl.ds(cut[0], cut[1] - cut[0])]
    if tile * TILE >= PLANE_ROWS and cut[0] == 0:
        same = same_block(tile)
        local = weights[:, :NEAR]
        blank = jnp.zeros_like(local)
        far = jnp.concatenate([jnp.where(same, blank, local), weights[:, NEAR:]], axis=1)
        return dot_f32(far, part) + dot_f32(jnp.where(same, local, blank), near_values[...])
    return dot_f32(weights, part)


def lane_max(scores, former):
    for begin in range(0, scores.shape[1], HEAD_DIM):
        piece = scores[:, begin : begin + HEAD_DIM]
        former = piece if former is None else jnp.maximum(former, piece)
    return former


def weigh(scores, top):
    return jnp.exp2((scores - top) * EXP_SCALE).astype(jnp.bfloat16)


def run_tiles(score_parts, sum_parts, start_top, finish_tile):
    former = None
    for tile in range(TILES + 1):
        scores, lanes, sums = [], None, None
        for index in range(len(score_parts)):
            if tile < TILES:
                part = score_parts[index](tile)
                lanes = lane_max(part, lanes)
                scores.append(part)
            if former is not None:
                part = sum_parts[index](weigh(former[0][index], former[1]), tile - 1)
                sums = part if sums is None else sums + part
        if former is not None:
            finish_tile(tile - 1, former[1], sums)
        if tile < TILES:
            top = jnp.max(lanes, axis=1, keepdims=True)
            former = (scores, start_top(tile, top))


def first_kernel(queries, mine, sums, tops, values, near_values):
    beside_ones(values, mine[pl.ds(HALF, HALF)])
    beside_ones(near_values, mine[pl.ds(NEAR_AT + PLANE_ROWS, NEAR)])

    def finish_tile(tile, top, total):
        sums[tile_rows(tile)] = total
        tops[tile_rows(tile)] = jnp.broadcast_to(top, (TILE, HEAD_DIM))

    run_tiles(
        [lambda tile, cut=cut: half_scores(queries, mine, tile, cut) for cut in CUTS],
        [
            lambda weights, tile, cut=cut: half_sums(weights, values, near_values, tile, cut)
            for cut in CUTS
        ],
        lambda tile, top: top,
        finish_tile,
    )


def second_kernel(
    length, queries, mine, theirs, sums, tops, out, values, near_values, text, text_values, done
):
    here = head_slot() // GROUP_HEADS == lax.axis_index("c")

    @pl.when(here)
    def _():
        text[...] = mine[pl.ds(TEXT_AT, EXTRA)]

    @pl.when(jnp.logical_not(here))
    def _():
        text[...] = theirs[pl.ds(TEXT_AT, EXTRA)]

    beside_ones(values, theirs[pl.ds(HALF, HALF)])
    beside_ones(near_values, theirs[pl.ds(NEAR_AT + PLANE_ROWS, NEAR)])
    beside_ones(text_values, text[pl.ds(TEXT, TEXT)])
    parts = text[pl.ds(2 * TEXT, 16)].astype(jnp.float32)
    live = lax.broadcasted_iota(jnp.int32, (1, TEXT), 1) < length[0]

    def text_scores(tile):
        scores = dot_t_f32(queries[tile_rows(tile)], text[pl.ds(0, TEXT)])
        return jnp.where(live, scores, -1e30)

    def start_top(tile, top):
        return jnp.maximum(tops[tile_rows(tile), 0:1], top)

    def finish_tile(tile, top, total):
        former = jnp.exp2((tops[tile_rows(tile), 0:1] - top) * EXP_SCALE)
        total = total + sums[tile_rows(tile)] * former
        step = tile * TILE // PLANE_ROWS
        gate = parts[3 * step : 3 * step + 1] + parts[3 * step + 1 : 3 * step + 2]
        gate = gate + parts[3 * step + 2 : 3 * step + 3]
        attended = total[:, :HEAD_DIM] / total[:, HEAD_DIM:]
        done[tile_rows(tile)] = (gate * attended).astype(jnp.bfloat16)

    run_tiles(
        [lambda tile, cut=cut: half_scores(queries, theirs, tile, cut) for cut in CUTS]
        + [text_scores],
        [
            lambda weights, tile, cut=cut: half_sums(weights, values, near_values, tile, cut)
            for cut in CUTS
        ]
        + [lambda weights, tile: dot_f32(weights, text_values[...])],
        start_top,
        finish_tile,
    )
    row = lax.broadcasted_iota(jnp.int32, (16 * BACK, 80), 0)
    column = lax.broadcasted_iota(jnp.int32, (16 * BACK, 80), 1)
    entry = row % BACK
    begin = (row // BACK) * ROWS
    place_first = one_hot((column == begin + entry) & (entry < ROWS))
    place_second = one_hot((column == begin + entry - 8) & (entry >= 8) & (entry < 8 + ROWS))
    for part in range(4):
        message = dot_f32(place_first, done[pl.ds(part * 80, 80)])
        message += dot_f32(place_second, done[pl.ds(PLANE_ROWS + part * 80, 80)])
        out[pl.ds(part * 16, 16)] = message.astype(jnp.bfloat16).reshape(16, BACK, HEAD_DIM)


def first_pass(queries, mine):
    vmem = pl.BlockSpec(memory_space=pltpu.VMEM)
    return pl.pallas_call(
        first_kernel,
        out_shape=(
            jax.ShapeDtypeStruct((2 * PLANE_ROWS, 2 * HEAD_DIM), jnp.float32),
            jax.ShapeDtypeStruct((2 * PLANE_ROWS, HEAD_DIM), jnp.float32),
        ),
        in_specs=[vmem, vmem],
        out_specs=(vmem, vmem),
        scratch_shapes=[
            pltpu.VMEM((HALF, 2 * HEAD_DIM), jnp.bfloat16),
            pltpu.VMEM((NEAR, 2 * HEAD_DIM), jnp.bfloat16),
        ],
        cost_estimate=pl.CostEstimate(
            flops=4 * 640 * 1600 * HEAD_DIM, bytes_accessed=2 * SHARED * HEAD_DIM, transcendentals=640 * HALF
        ),
        compiler_params=pltpu.CompilerParams(vmem_limit_bytes=VMEM_LIMIT),
    )(queries, mine)


def second_pass(text_length, queries, mine, theirs, sums, tops):
    vmem = pl.BlockSpec(memory_space=pltpu.VMEM)
    return pl.pallas_call(
        second_kernel,
        out_shape=jax.ShapeDtypeStruct((PEERS, BACK, HEAD_DIM), jnp.bfloat16),
        in_specs=[pl.BlockSpec(memory_space=pltpu.SMEM)] + [vmem] * 5,
        out_specs=vmem,
        scratch_shapes=[
            pltpu.VMEM((HALF, 2 * HEAD_DIM), jnp.bfloat16),
            pltpu.VMEM((NEAR, 2 * HEAD_DIM), jnp.bfloat16),
            pltpu.VMEM((EXTRA, HEAD_DIM), jnp.bfloat16),
            pltpu.VMEM((TEXT, 2 * HEAD_DIM), jnp.bfloat16),
            pltpu.VMEM((2 * PLANE_ROWS, HEAD_DIM), jnp.bfloat16),
        ],
        compiler_params=pltpu.CompilerParams(vmem_limit_bytes=VMEM_LIMIT),
    )(text_length, queries, mine, theirs, sums, tops)


def finish_kernel(messages, first, second):
    for rank in range(ACTIVE):
        head = (rank % 4) * PAIR_HEADS + rank // 4
        columns = pl.ds(head * HEAD_DIM, HEAD_DIM)
        message = messages[rank]
        first[:, columns] = message[0:ROWS]
        second[:, columns] = message[8 : 8 + ROWS]


def finish(messages):
    shape = jax.ShapeDtypeStruct((ROWS, HEADS * HEAD_DIM), jnp.bfloat16)
    return pl.pallas_call(
        finish_kernel,
        out_shape=(shape, shape),
        compiler_params=pltpu.CompilerParams(vmem_limit_bytes=VMEM_LIMIT),
    )(messages)


def body(
    query_first,
    keys_first,
    values_first,
    query_second,
    keys_second,
    values_second,
    text_keys,
    text_values,
    gate_table,
    timesteps,
    text_length,
):
    sent, extra = pack(
        keys_first,
        values_first,
        query_first,
        query_second,
        keys_second,
        values_second,
        text_keys,
        text_values,
        gate_table,
        timesteps,
    )
    arrived = lax.all_to_all(sent, PLANE, 0, 0, tiled=True)
    copies, queries, near = unpack(arrived)
    planes = lax.all_to_all(copies, "x", 0, 0, tiled=True)
    mine = join(planes, near, extra)
    theirs = lax.ppermute(mine, "c", [(0, 1), (1, 0)])
    sums, tops = first_pass(queries, mine)
    back = second_pass(text_length, queries, mine, theirs, sums, tops)
    returned = lax.all_to_all(back, PLANE, 0, 0, tiled=True)
    return finish(returned)


def solution(mesh):
    fine = Mesh(mesh.devices.reshape(8, 4, 2, 4, 2), AXES)
    rows = P(AXES, None)
    heads = P(None, ("yh", "c"))
    return jax.shard_map(
        body,
        mesh=fine,
        in_specs=(rows,) * 6 + (heads,) * 3 + (P(), P()),
        out_specs=(rows, rows),
        check_vma=False,
    )
```

```python
import jax
import jax.numpy as jnp
import numpy as np
from jax import lax
from jax.experimental import pallas as pl
from jax.experimental.pallas import tpu as pltpu
from jax.sharding import Mesh
from jax.sharding import PartitionSpec as P

HEAD_DIM = 128
HEADS = 40
GROUP_HEADS = 5
PAIR_HEADS = 10
ROWS = 5
PLANE_ROWS = 320
BLOCK_ROWS = 20
PEERS = 64
CHUNK = 32
BACK = 2 * ROWS
TEXT = 512
EXP_SCALE = float(HEAD_DIM ** (-0.5) * np.log2(np.e))

AXES = ("z", "x", "yl", "yh", "c")
PLANE = ("z", "yl", "yh")
ACTIVE = 4 * PAIR_HEADS

HALF = 4 * PLANE_ROWS
NEAR_AT = 2 * HALF
TEXT_AT = NEAR_AT + 2 * PLANE_ROWS
GATE_AT = TEXT_AT + 2 * TEXT
SHARED = GATE_AT + 16
EXTRA = SHARED - TEXT_AT

VMEM_LIMIT = 48 * 1024 * 1024


def dot_f32(left, right):
    return lax.dot_general(
        left, right, (((1,), (0,)), ((), ())), preferred_element_type=jnp.float32
    )


def dot_t_f32(left, right):
    return lax.dot_general(
        left, right, (((1,), (1,)), ((), ())), preferred_element_type=jnp.float32
    )


def head_slot():
    return lax.axis_index("z") * 2 + lax.axis_index("yl")


def in_hbm(array):
    return pltpu.with_memory_space_constraint(array, pltpu.HBM)


def one_hot(condition):
    return jnp.where(condition, 1.0, 0.0).astype(jnp.bfloat16)


def pack_kernel(
    k1, v1, q1, q2, k2, v2, text_k, text_v, gates, steps, out, extra, held, gate, step_ids, sems
):
    slot = lax.rem(head_slot(), GROUP_HEADS)
    columns = pl.ds(pl.multiple_of(slot * HEAD_DIM, HEAD_DIM), HEAD_DIM)
    targets = [(array, held.at[index]) for index, array in enumerate((k1, v1, q1, q2, k2, v2))]
    targets += [
        (steps, step_ids),
        (gates.at[:, columns], gate),
        (text_k.at[:, columns], extra.at[pl.ds(0, TEXT)]),
        (text_v.at[:, columns], extra.at[pl.ds(TEXT, TEXT)]),
    ]
    fetches = [
        pltpu.make_async_copy(source, target, sems.at[index])
        for index, (source, target) in enumerate(targets)
    ]
    for fetch in fetches:
        fetch.start()
    total = None
    for index in range(6):
        row = lax.broadcasted_iota(jnp.int32, (CHUNK, ROWS), 0)
        column = lax.broadcasted_iota(jnp.int32, (CHUNK, ROWS), 1)
        fetches[index].wait()
        part = dot_f32(one_hot(row == column + index * ROWS), held[index])
        total = part if total is None else total + part
    packed = total.astype(jnp.bfloat16)
    for rank in range(PEERS):
        if rank < ACTIVE:
            head = (rank % 4) * PAIR_HEADS + rank // 4
            out[rank] = packed[:, head * HEAD_DIM : (head + 1) * HEAD_DIM]
        else:
            out[rank] = jnp.zeros((CHUNK, HEAD_DIM), jnp.bfloat16)
    for fetch in fetches[6:]:
        fetch.wait()
    row = lax.broadcasted_iota(jnp.int32, (16, HEAD_DIM), 0)
    parts = jnp.zeros((16, HEAD_DIM), jnp.float32)
    for step in range(2):
        left = gate[pl.ds(step_ids[step], 1), :]
        for index in range(3):
            part = left.astype(jnp.bfloat16).astype(jnp.float32)
            parts = jnp.where(row == step * 3 + index, part, parts)
            left = left - part
    extra[pl.ds(2 * TEXT, 16)] = parts.astype(jnp.bfloat16)


def pack(*arrays):
    vmem = pl.BlockSpec(memory_space=pltpu.VMEM)
    return pl.pallas_call(
        pack_kernel,
        out_shape=(
            jax.ShapeDtypeStruct((PEERS, CHUNK, HEAD_DIM), jnp.bfloat16),
            jax.ShapeDtypeStruct((EXTRA, HEAD_DIM), jnp.bfloat16),
        ),
        in_specs=[pl.BlockSpec(memory_space=pltpu.HBM)] * 10,
        out_specs=(vmem, vmem),
        scratch_shapes=[
            pltpu.VMEM((6, ROWS, HEADS * HEAD_DIM), jnp.bfloat16),
            pltpu.VMEM((35, HEAD_DIM), jnp.float32),
            pltpu.SMEM((2,), jnp.int32),
            pltpu.SemaphoreType.DMA((10,)),
        ],
        compiler_params=pltpu.CompilerParams(vmem_limit_bytes=VMEM_LIMIT),
    )(*[in_hbm(array) for array in arrays])


def unpack_kernel(messages, copies, queries, near):
    source = lax.broadcasted_iota(jnp.int32, (1, 256), 1)
    message, entry = source // CHUNK, source % CHUNK
    target = entry + ((entry * 13) // 64) * 35 + message * ROWS
    order = one_hot(lax.broadcasted_iota(jnp.int32, (240, 256), 0) == target)
    for step in range(8):
        rows = messages[pl.ds(step * 8, 8)].reshape(256, HEAD_DIM)
        ordered = dot_f32(order, rows).astype(jnp.bfloat16)
        for array in range(6):
            piece = ordered[array * 40 : (array + 1) * 40]
            place = pl.ds((array % 2) * PLANE_ROWS + step * 40, 40)
            if array < 2:
                for copy in range(4):
                    copies[copy, place] = piece
            elif array < 4:
                queries[place] = piece
            else:
                near[place] = piece


def unpack(messages):
    rows = jax.ShapeDtypeStruct((2 * PLANE_ROWS, HEAD_DIM), jnp.bfloat16)
    return pl.pallas_call(
        unpack_kernel,
        out_shape=(
            jax.ShapeDtypeStruct((4, 2 * PLANE_ROWS, HEAD_DIM), jnp.bfloat16),
            rows,
            rows,
        ),
        compiler_params=pltpu.CompilerParams(vmem_limit_bytes=VMEM_LIMIT),
    )(messages)


def join_kernel(planes, near, extra, out):
    own = lax.axis_index("x")
    for place in range(4):
        source = lax.rem(own + place, 4)
        for part in range(2):
            out[pl.ds(part * HALF + place * PLANE_ROWS, PLANE_ROWS)] = planes[
                source, pl.ds(part * PLANE_ROWS, PLANE_ROWS)
            ]
    out[pl.ds(NEAR_AT, 2 * PLANE_ROWS)] = near[...]
    out[pl.ds(TEXT_AT, EXTRA)] = extra[...]


def join(planes, near, extra):
    return pl.pallas_call(
        join_kernel,
        out_shape=jax.ShapeDtypeStruct((SHARED, HEAD_DIM), jnp.bfloat16),
        compiler_params=pltpu.CompilerParams(vmem_limit_bytes=VMEM_LIMIT),
    )(planes, near, extra)


TILE = 160
TILES = 2 * PLANE_ROWS // TILE
NEAR = 384
CUTS = ((0, 512), (512, 1024), (1024, HALF))


def block_of(index):
    return jnp.floor((index.astype(jnp.float32) + 0.5) * (1.0 / BLOCK_ROWS))


def beside_ones(target, rows):
    target[:, :HEAD_DIM] = rows
    target[:, HEAD_DIM:] = jnp.ones_like(rows)


def same_block(tile):
    row = lax.broadcasted_iota(jnp.int32, (TILE, 1), 0) + (tile * TILE) % PLANE_ROWS
    column = lax.broadcasted_iota(jnp.int32, (1, NEAR), 1)
    return block_of(row) == block_of(column)


def tile_rows(tile):
    return pl.ds(tile * TILE, TILE)


def half_scores(queries, keys, tile, cut):
    rows = queries[tile_rows(tile)]
    scores = dot_t_f32(rows, keys[pl.ds(cut[0], cut[1] - cut[0])])
    if tile * TILE >= PLANE_ROWS and cut[0] == 0:
        near = dot_t_f32(rows, keys[pl.ds(NEAR_AT, NEAR)])
        near = jnp.where(same_block(tile), near, scores[:, :NEAR])
        scores = jnp.concatenate([near, scores[:, NEAR:]], axis=1)
    return scores


def half_sums(weights, values, near_values, tile, cut):
    part = values[pl.ds(cut[0], cut[1] - cut[0])]
    if tile * TILE >= PLANE_ROWS and cut[0] == 0:
        same = same_block(tile)
        local = weights[:, :NEAR]
        blank = jnp.zeros_like(local)
        far = jnp.concatenate([jnp.where(same, blank, local), weights[:, NEAR:]], axis=1)
        return dot_f32(far, part) + dot_f32(jnp.where(same, local, blank), near_values[...])
    return dot_f32(weights, part)


def lane_max(scores, former):
    for begin in range(0, scores.shape[1], HEAD_DIM):
        piece = scores[:, begin : begin + HEAD_DIM]
        former = piece if former is None else jnp.maximum(former, piece)
    return former


def weigh(scores, top):
    return jnp.exp2((scores - top) * EXP_SCALE).astype(jnp.bfloat16)


def run_tiles(score_parts, sum_parts, start_top, finish_tile):
    former = None
    for tile in range(TILES + 1):
        scores, lanes, sums = [], None, None
        for index in range(len(score_parts)):
            if tile < TILES:
                part = score_parts[index](tile)
                lanes = lane_max(part, lanes)
                scores.append(part)
            if former is not None:
                part = sum_parts[index](weigh(former[0][index], former[1]), tile - 1)
                sums = part if sums is None else sums + part
        if former is not None:
            finish_tile(tile - 1, former[1], sums)
        if tile < TILES:
            top = jnp.max(lanes, axis=1, keepdims=True)
            former = (scores, start_top(tile, top))


def first_kernel(queries, mine, sums, tops, values, near_values):
    beside_ones(values, mine[pl.ds(HALF, HALF)])
    beside_ones(near_values, mine[pl.ds(NEAR_AT + PLANE_ROWS, NEAR)])

    def finish_tile(tile, top, total):
        sums[tile_rows(tile)] = total
        tops[tile_rows(tile)] = jnp.broadcast_to(top, (TILE, HEAD_DIM))

    run_tiles(
        [lambda tile, cut=cut: half_scores(queries, mine, tile, cut) for cut in CUTS],
        [
            lambda weights, tile, cut=cut: half_sums(weights, values, near_values, tile, cut)
            for cut in CUTS
        ],
        lambda tile, top: top,
        finish_tile,
    )


def second_kernel(
    length, queries, mine, theirs, sums, tops, out, values, near_values, text, text_values, done
):
    here = head_slot() // GROUP_HEADS == lax.axis_index("c")

    @pl.when(here)
    def _():
        text[...] = mine[pl.ds(TEXT_AT, EXTRA)]

    @pl.when(jnp.logical_not(here))
    def _():
        text[...] = theirs[pl.ds(TEXT_AT, EXTRA)]

    beside_ones(values, theirs[pl.ds(HALF, HALF)])
    beside_ones(near_values, theirs[pl.ds(NEAR_AT + PLANE_ROWS, NEAR)])
    beside_ones(text_values, text[pl.ds(TEXT, TEXT)])
    parts = text[pl.ds(2 * TEXT, 16)].astype(jnp.float32)
    live = lax.broadcasted_iota(jnp.int32, (1, TEXT), 1) < length[0]

    def text_scores(tile):
        scores = dot_t_f32(queries[tile_rows(tile)], text[pl.ds(0, TEXT)])
        return jnp.where(live, scores, -1e30)

    def start_top(tile, top):
        return jnp.maximum(tops[tile_rows(tile), 0:1], top)

    def finish_tile(tile, top, total):
        former = jnp.exp2((tops[tile_rows(tile), 0:1] - top) * EXP_SCALE)
        total = total + sums[tile_rows(tile)] * former
        step = tile * TILE // PLANE_ROWS
        gate = parts[3 * step : 3 * step + 1] + parts[3 * step + 1 : 3 * step + 2]
        gate = gate + parts[3 * step + 2 : 3 * step + 3]
        attended = total[:, :HEAD_DIM] / total[:, HEAD_DIM:]
        done[tile_rows(tile)] = (gate * attended).astype(jnp.bfloat16)

    run_tiles(
        [lambda tile, cut=cut: half_scores(queries, theirs, tile, cut) for cut in CUTS]
        + [text_scores],
        [
            lambda weights, tile, cut=cut: half_sums(weights, values, near_values, tile, cut)
            for cut in CUTS
        ]
        + [lambda weights, tile: dot_f32(weights, text_values[...])],
        start_top,
        finish_tile,
    )
    row = lax.broadcasted_iota(jnp.int32, (160, 80), 0)
    column = lax.broadcasted_iota(jnp.int32, (160, 80), 1)
    place_first = one_hot(row == 2 * column)
    place_second = one_hot(row == 2 * column + 1)
    for part in range(4):
        rows = dot_f32(place_first, done[pl.ds(part * 80, 80)])
        rows += dot_f32(place_second, done[pl.ds(PLANE_ROWS + part * 80, 80)])
        out[pl.ds(part * 160, 160)] = rows.astype(jnp.bfloat16)


def first_pass(queries, mine):
    vmem = pl.BlockSpec(memory_space=pltpu.VMEM)
    return pl.pallas_call(
        first_kernel,
        out_shape=(
            jax.ShapeDtypeStruct((2 * PLANE_ROWS, 2 * HEAD_DIM), jnp.float32),
            jax.ShapeDtypeStruct((2 * PLANE_ROWS, HEAD_DIM), jnp.float32),
        ),
        in_specs=[vmem, vmem],
        out_specs=(vmem, vmem),
        scratch_shapes=[
            pltpu.VMEM((HALF, 2 * HEAD_DIM), jnp.bfloat16),
            pltpu.VMEM((NEAR, 2 * HEAD_DIM), jnp.bfloat16),
        ],
        cost_estimate=pl.CostEstimate(
            flops=4 * 640 * 1600 * HEAD_DIM, bytes_accessed=2 * SHARED * HEAD_DIM, transcendentals=640 * HALF
        ),
        compiler_params=pltpu.CompilerParams(vmem_limit_bytes=VMEM_LIMIT),
    )(queries, mine)


def second_pass(text_length, queries, mine, theirs, sums, tops):
    vmem = pl.BlockSpec(memory_space=pltpu.VMEM)
    return pl.pallas_call(
        second_kernel,
        out_shape=jax.ShapeDtypeStruct((PEERS * BACK, HEAD_DIM), jnp.bfloat16),
        in_specs=[pl.BlockSpec(memory_space=pltpu.SMEM)] + [vmem] * 5,
        out_specs=vmem,
        scratch_shapes=[
            pltpu.VMEM((HALF, 2 * HEAD_DIM), jnp.bfloat16),
            pltpu.VMEM((NEAR, 2 * HEAD_DIM), jnp.bfloat16),
            pltpu.VMEM((EXTRA, HEAD_DIM), jnp.bfloat16),
            pltpu.VMEM((TEXT, 2 * HEAD_DIM), jnp.bfloat16),
            pltpu.VMEM((2 * PLANE_ROWS, HEAD_DIM), jnp.bfloat16),
        ],
        compiler_params=pltpu.CompilerParams(vmem_limit_bytes=VMEM_LIMIT),
    )(text_length, queries, mine, theirs, sums, tops)


def finish_kernel(messages, first, second):
    source = lax.broadcasted_iota(jnp.int32, (1, 8 * BACK), 1)
    message = (source * 205) // 2048
    entry = source - message * BACK
    target = message * 16 + (entry % 2) * 8 + entry // 2
    order = one_hot(lax.broadcasted_iota(jnp.int32, (128, 8 * BACK), 0) == target)
    for part in range(ACTIVE // 8):
        rows = dot_f32(order, messages[pl.ds(part * 8 * BACK, 8 * BACK)]).astype(jnp.bfloat16)
        for index in range(8):
            rank = part * 8 + index
            head = (rank % 4) * PAIR_HEADS + rank // 4
            columns = pl.ds(head * HEAD_DIM, HEAD_DIM)
            first[:, columns] = rows[index * 16 : index * 16 + ROWS]
            second[:, columns] = rows[index * 16 + 8 : index * 16 + 8 + ROWS]


def finish(messages):
    shape = jax.ShapeDtypeStruct((ROWS, HEADS * HEAD_DIM), jnp.bfloat16)
    return pl.pallas_call(
        finish_kernel,
        out_shape=(shape, shape),
        compiler_params=pltpu.CompilerParams(vmem_limit_bytes=VMEM_LIMIT),
    )(messages)


def body(
    query_first,
    keys_first,
    values_first,
    query_second,
    keys_second,
    values_second,
    text_keys,
    text_values,
    gate_table,
    timesteps,
    text_length,
):
    sent, extra = pack(
        keys_first,
        values_first,
        query_first,
        query_second,
        keys_second,
        values_second,
        text_keys,
        text_values,
        gate_table,
        timesteps,
    )
    arrived = lax.all_to_all(sent, PLANE, 0, 0, tiled=True)
    copies, queries, near = unpack(arrived)
    planes = lax.all_to_all(copies, "x", 0, 0, tiled=True)
    mine = join(planes, near, extra)
    theirs = lax.ppermute(mine, "c", [(0, 1), (1, 0)])
    sums, tops = first_pass(queries, mine)
    back = second_pass(text_length, queries, mine, theirs, sums, tops)
    pairs = back.reshape(PEERS, ROWS, 2, HEAD_DIM)
    returned = lax.all_to_all(pairs, PLANE, 0, 0, tiled=True)
    return finish(returned.reshape(PEERS * BACK, HEAD_DIM))


def solution(mesh):
    fine = Mesh(mesh.devices.reshape(8, 4, 2, 4, 2), AXES)
    rows = P(AXES, None)
    heads = P(None, ("yh", "c"))
    return jax.shard_map(
        body,
        mesh=fine,
        in_specs=(rows,) * 6 + (heads,) * 3 + (P(), P()),
        out_specs=(rows, rows),
        check_vma=False,
    )
```

```python
import jax
import jax.numpy as jnp
import numpy as np
from jax import lax
from jax.experimental import pallas as pl
from jax.experimental.pallas import tpu as pltpu
from jax.sharding import Mesh
from jax.sharding import PartitionSpec as P

HEAD_DIM = 128
HEADS = 40
GROUP_HEADS = 5
PAIR_HEADS = 10
ROWS = 5
PLANE_ROWS = 320
BLOCK_ROWS = 20
PEERS = 64
CHUNK = 6 * ROWS
BACK = 2 * ROWS
TEXT = 512
EXP_SCALE = float(HEAD_DIM ** (-0.5) * np.log2(np.e))

AXES = ("z", "x", "yl", "yh", "c")
PLANE = ("z", "yl", "yh")
ACTIVE = 4 * PAIR_HEADS

HALF = 4 * PLANE_ROWS
NEAR_AT = 2 * HALF
TEXT_AT = NEAR_AT + 2 * PLANE_ROWS
GATE_AT = TEXT_AT + 2 * TEXT
SHARED = GATE_AT + 16
EXTRA = SHARED - TEXT_AT

VMEM_LIMIT = 48 * 1024 * 1024


def dot_f32(left, right):
    return lax.dot_general(
        left, right, (((1,), (0,)), ((), ())), preferred_element_type=jnp.float32
    )


def dot_t_f32(left, right):
    return lax.dot_general(
        left, right, (((1,), (1,)), ((), ())), preferred_element_type=jnp.float32
    )


def head_slot():
    return lax.axis_index("z") * 2 + lax.axis_index("yl")


def in_hbm(array):
    return pltpu.with_memory_space_constraint(array, pltpu.HBM)


def one_hot(condition):
    return jnp.where(condition, 1.0, 0.0).astype(jnp.bfloat16)


def message_of(source, rows):
    return (source * (65536 // rows + 1)) // 65536


def pack_kernel(
    k1, v1, q1, q2, k2, v2, text_k, text_v, gates, steps, out, extra,
    held, stacked, gate, step_ids, sems,
):
    slot = lax.rem(head_slot(), GROUP_HEADS)
    columns = pl.ds(pl.multiple_of(slot * HEAD_DIM, HEAD_DIM), HEAD_DIM)
    targets = [(array, held.at[index]) for index, array in enumerate((k1, v1, q1, q2, k2, v2))]
    targets += [
        (steps, step_ids),
        (gates.at[:, columns], gate),
        (text_k.at[:, columns], extra.at[pl.ds(0, TEXT)]),
        (text_v.at[:, columns], extra.at[pl.ds(TEXT, TEXT)]),
    ]
    fetches = [
        pltpu.make_async_copy(source, target, sems.at[index])
        for index, (source, target) in enumerate(targets)
    ]
    for fetch in fetches:
        fetch.start()
    stacked[...] = jnp.zeros_like(stacked)
    for index in range(6):
        fetches[index].wait()
        stacked[pl.ds(index * 8, ROWS)] = held[index]
    source = lax.broadcasted_iota(jnp.int32, (1, 8 * 48), 1)
    message = message_of(source, 48)
    array = (source - message * 48) // 8
    entry = source - message * 48 - array * 8
    target = jnp.where(entry < ROWS, message * CHUNK + array * ROWS + entry, -1)
    order = one_hot(lax.broadcasted_iota(jnp.int32, (8 * CHUNK, 8 * 48), 0) == target)
    for part in range(PEERS // 8):
        place = pl.ds(part * 8 * CHUNK, 8 * CHUNK)
        if part * 8 >= ACTIVE:
            out[place] = jnp.zeros((8 * CHUNK, HEAD_DIM), jnp.bfloat16)
            continue
        pieces = []
        for rank in range(part * 8, part * 8 + 8):
            head = (rank % 4) * PAIR_HEADS + rank // 4
            pieces.append(stacked[:, head * HEAD_DIM : (head + 1) * HEAD_DIM])
        out[place] = dot_f32(order, jnp.concatenate(pieces, axis=0)).astype(jnp.bfloat16)
    for fetch in fetches[6:]:
        fetch.wait()
    row = lax.broadcasted_iota(jnp.int32, (16, HEAD_DIM), 0)
    parts = jnp.zeros((16, HEAD_DIM), jnp.float32)
    for step in range(2):
        left = gate[pl.ds(step_ids[step], 1), :]
        for index in range(3):
            part = left.astype(jnp.bfloat16).astype(jnp.float32)
            parts = jnp.where(row == step * 3 + index, part, parts)
            left = left - part
    extra[pl.ds(2 * TEXT, 16)] = parts.astype(jnp.bfloat16)


def pack(*arrays):
    vmem = pl.BlockSpec(memory_space=pltpu.VMEM)
    return pl.pallas_call(
        pack_kernel,
        out_shape=(
            jax.ShapeDtypeStruct((PEERS * CHUNK, HEAD_DIM), jnp.bfloat16),
            jax.ShapeDtypeStruct((EXTRA, HEAD_DIM), jnp.bfloat16),
        ),
        in_specs=[pl.BlockSpec(memory_space=pltpu.HBM)] * 10,
        out_specs=(vmem, vmem),
        scratch_shapes=[
            pltpu.VMEM((6, ROWS, HEADS * HEAD_DIM), jnp.bfloat16),
            pltpu.VMEM((48, HEADS * HEAD_DIM), jnp.bfloat16),
            pltpu.VMEM((35, HEAD_DIM), jnp.float32),
            pltpu.SMEM((2,), jnp.int32),
            pltpu.SemaphoreType.DMA((10,)),
        ],
        compiler_params=pltpu.CompilerParams(vmem_limit_bytes=VMEM_LIMIT),
    )(*[in_hbm(array) for array in arrays])


def unpack_kernel(messages, copies, queries, near):
    source = lax.broadcasted_iota(jnp.int32, (1, 8 * CHUNK), 1)
    message = message_of(source, CHUNK)
    entry = source - message * CHUNK
    target = entry + ((entry * 13) // 64) * 35 + message * ROWS
    order = one_hot(lax.broadcasted_iota(jnp.int32, (240, 8 * CHUNK), 0) == target)
    for step in range(8):
        rows = messages[pl.ds(step * 8 * CHUNK, 8 * CHUNK)]
        ordered = dot_f32(order, rows).astype(jnp.bfloat16)
        for array in range(6):
            piece = ordered[array * 40 : (array + 1) * 40]
            place = pl.ds((array % 2) * PLANE_ROWS + step * 40, 40)
            if array < 2:
                for copy in range(4):
                    copies[copy, place] = piece
            elif array < 4:
                queries[place] = piece
            else:
                near[place] = piece


def unpack(messages):
    rows = jax.ShapeDtypeStruct((2 * PLANE_ROWS, HEAD_DIM), jnp.bfloat16)
    return pl.pallas_call(
        unpack_kernel,
        out_shape=(
            jax.ShapeDtypeStruct((4, 2 * PLANE_ROWS, HEAD_DIM), jnp.bfloat16),
            rows,
            rows,
        ),
        compiler_params=pltpu.CompilerParams(vmem_limit_bytes=VMEM_LIMIT),
    )(messages)


def join_kernel(planes, near, extra, out):
    own = lax.axis_index("x")
    for place in range(4):
        source = lax.rem(own + place, 4)
        for part in range(2):
            out[pl.ds(part * HALF + place * PLANE_ROWS, PLANE_ROWS)] = planes[
                source, pl.ds(part * PLANE_ROWS, PLANE_ROWS)
            ]
    out[pl.ds(NEAR_AT, 2 * PLANE_ROWS)] = near[...]
    out[pl.ds(TEXT_AT, EXTRA)] = extra[...]


def join(planes, near, extra):
    return pl.pallas_call(
        join_kernel,
        out_shape=jax.ShapeDtypeStruct((SHARED, HEAD_DIM), jnp.bfloat16),
        compiler_params=pltpu.CompilerParams(vmem_limit_bytes=VMEM_LIMIT),
    )(planes, near, extra)


TILE = 160
TILES = 2 * PLANE_ROWS // TILE
NEAR = 384
CUTS = ((0, 512), (512, 1024), (1024, HALF))


def block_of(index):
    return jnp.floor((index.astype(jnp.float32) + 0.5) * (1.0 / BLOCK_ROWS))


def beside_ones(target, rows):
    target[:, :HEAD_DIM] = rows
    target[:, HEAD_DIM:] = jnp.ones_like(rows)


def same_block(tile):
    row = lax.broadcasted_iota(jnp.int32, (TILE, 1), 0) + (tile * TILE) % PLANE_ROWS
    column = lax.broadcasted_iota(jnp.int32, (1, NEAR), 1)
    return block_of(row) == block_of(column)


def tile_rows(tile):
    return pl.ds(tile * TILE, TILE)


def half_scores(queries, keys, tile, cut):
    rows = queries[tile_rows(tile)]
    scores = dot_t_f32(rows, keys[pl.ds(cut[0], cut[1] - cut[0])])
    if tile * TILE >= PLANE_ROWS and cut[0] == 0:
        near = dot_t_f32(rows, keys[pl.ds(NEAR_AT, NEAR)])
        near = jnp.where(same_block(tile), near, scores[:, :NEAR])
        scores = jnp.concatenate([near, scores[:, NEAR:]], axis=1)
    return scores


def half_sums(weights, values, near_values, tile, cut):
    part = values[pl.ds(cut[0], cut[1] - cut[0])]
    if tile * TILE >= PLANE_ROWS and cut[0] == 0:
        same = same_block(tile)
        local = weights[:, :NEAR]
        blank = jnp.zeros_like(local)
        far = jnp.concatenate([jnp.where(same, blank, local), weights[:, NEAR:]], axis=1)
        return dot_f32(far, part) + dot_f32(jnp.where(same, local, blank), near_values[...])
    return dot_f32(weights, part)


def lane_max(scores, former):
    for begin in range(0, scores.shape[1], HEAD_DIM):
        piece = scores[:, begin : begin + HEAD_DIM]
        former = piece if former is None else jnp.maximum(former, piece)
    return former


def weigh(scores, top):
    return jnp.exp2((scores - top) * EXP_SCALE).astype(jnp.bfloat16)


def run_tiles(score_parts, sum_parts, start_top, finish_tile):
    former = None
    for tile in range(TILES + 1):
        scores, lanes, sums = [], None, None
        for index in range(len(score_parts)):
            if tile < TILES:
                part = score_parts[index](tile)
                lanes = lane_max(part, lanes)
                scores.append(part)
            if former is not None:
                part = sum_parts[index](weigh(former[0][index], former[1]), tile - 1)
                sums = part if sums is None else sums + part
        if former is not None:
            finish_tile(tile - 1, former[1], sums)
        if tile < TILES:
            top = jnp.max(lanes, axis=1, keepdims=True)
            former = (scores, start_top(tile, top))


def first_kernel(queries, mine, sums, tops, values, near_values):
    beside_ones(values, mine[pl.ds(HALF, HALF)])
    beside_ones(near_values, mine[pl.ds(NEAR_AT + PLANE_ROWS, NEAR)])

    def finish_tile(tile, top, total):
        sums[tile_rows(tile)] = total
        tops[tile_rows(tile)] = jnp.broadcast_to(top, (TILE, HEAD_DIM))

    run_tiles(
        [lambda tile, cut=cut: half_scores(queries, mine, tile, cut) for cut in CUTS],
        [
            lambda weights, tile, cut=cut: half_sums(weights, values, near_values, tile, cut)
            for cut in CUTS
        ],
        lambda tile, top: top,
        finish_tile,
    )


def second_kernel(
    length, queries, mine, theirs, sums, tops, out, values, near_values, text, text_values, done
):
    here = head_slot() // GROUP_HEADS == lax.axis_index("c")

    @pl.when(here)
    def _():
        text[...] = mine[pl.ds(TEXT_AT, EXTRA)]

    @pl.when(jnp.logical_not(here))
    def _():
        text[...] = theirs[pl.ds(TEXT_AT, EXTRA)]

    beside_ones(values, theirs[pl.ds(HALF, HALF)])
    beside_ones(near_values, theirs[pl.ds(NEAR_AT + PLANE_ROWS, NEAR)])
    beside_ones(text_values, text[pl.ds(TEXT, TEXT)])
    parts = text[pl.ds(2 * TEXT, 16)].astype(jnp.float32)
    live = lax.broadcasted_iota(jnp.int32, (1, TEXT), 1) < length[0]

    def text_scores(tile):
        scores = dot_t_f32(queries[tile_rows(tile)], text[pl.ds(0, TEXT)])
        return jnp.where(live, scores, -1e30)

    def start_top(tile, top):
        return jnp.maximum(tops[tile_rows(tile), 0:1], top)

    def finish_tile(tile, top, total):
        former = jnp.exp2((tops[tile_rows(tile), 0:1] - top) * EXP_SCALE)
        total = total + sums[tile_rows(tile)] * former
        step = tile * TILE // PLANE_ROWS
        gate = parts[3 * step : 3 * step + 1] + parts[3 * step + 1 : 3 * step + 2]
        gate = gate + parts[3 * step + 2 : 3 * step + 3]
        attended = total[:, :HEAD_DIM] / total[:, HEAD_DIM:]
        done[tile_rows(tile)] = (gate * attended).astype(jnp.bfloat16)

    run_tiles(
        [lambda tile, cut=cut: half_scores(queries, theirs, tile, cut) for cut in CUTS]
        + [text_scores],
        [
            lambda weights, tile, cut=cut: half_sums(weights, values, near_values, tile, cut)
            for cut in CUTS
        ]
        + [lambda weights, tile: dot_f32(weights, text_values[...])],
        start_top,
        finish_tile,
    )
    row = lax.broadcasted_iota(jnp.int32, (160, 80), 0)
    column = lax.broadcasted_iota(jnp.int32, (160, 80), 1)
    place_first = one_hot(row == 2 * column)
    place_second = one_hot(row == 2 * column + 1)
    for part in range(4):
        rows = dot_f32(place_first, done[pl.ds(part * 80, 80)])
        rows += dot_f32(place_second, done[pl.ds(PLANE_ROWS + part * 80, 80)])
        out[pl.ds(part * 160, 160)] = rows.astype(jnp.bfloat16)


def first_pass(queries, mine):
    vmem = pl.BlockSpec(memory_space=pltpu.VMEM)
    return pl.pallas_call(
        first_kernel,
        out_shape=(
            jax.ShapeDtypeStruct((2 * PLANE_ROWS, 2 * HEAD_DIM), jnp.float32),
            jax.ShapeDtypeStruct((2 * PLANE_ROWS, HEAD_DIM), jnp.float32),
        ),
        in_specs=[vmem, vmem],
        out_specs=(vmem, vmem),
        scratch_shapes=[
            pltpu.VMEM((HALF, 2 * HEAD_DIM), jnp.bfloat16),
            pltpu.VMEM((NEAR, 2 * HEAD_DIM), jnp.bfloat16),
        ],
        cost_estimate=pl.CostEstimate(
            flops=4 * 640 * 1600 * HEAD_DIM, bytes_accessed=2 * SHARED * HEAD_DIM, transcendentals=640 * HALF
        ),
        compiler_params=pltpu.CompilerParams(vmem_limit_bytes=VMEM_LIMIT),
    )(queries, mine)


def second_pass(text_length, queries, mine, theirs, sums, tops):
    vmem = pl.BlockSpec(memory_space=pltpu.VMEM)
    return pl.pallas_call(
        second_kernel,
        out_shape=jax.ShapeDtypeStruct((PEERS * BACK, HEAD_DIM), jnp.bfloat16),
        in_specs=[pl.BlockSpec(memory_space=pltpu.SMEM)] + [vmem] * 5,
        out_specs=vmem,
        scratch_shapes=[
            pltpu.VMEM((HALF, 2 * HEAD_DIM), jnp.bfloat16),
            pltpu.VMEM((NEAR, 2 * HEAD_DIM), jnp.bfloat16),
            pltpu.VMEM((EXTRA, HEAD_DIM), jnp.bfloat16),
            pltpu.VMEM((TEXT, 2 * HEAD_DIM), jnp.bfloat16),
            pltpu.VMEM((2 * PLANE_ROWS, HEAD_DIM), jnp.bfloat16),
        ],
        compiler_params=pltpu.CompilerParams(vmem_limit_bytes=VMEM_LIMIT),
    )(text_length, queries, mine, theirs, sums, tops)


def finish_kernel(messages, first, second):
    source = lax.broadcasted_iota(jnp.int32, (1, 8 * BACK), 1)
    message = message_of(source, BACK)
    entry = source - message * BACK
    target = message * 16 + (entry % 2) * 8 + entry // 2
    order = one_hot(lax.broadcasted_iota(jnp.int32, (128, 8 * BACK), 0) == target)
    for part in range(ACTIVE // 8):
        rows = dot_f32(order, messages[pl.ds(part * 8 * BACK, 8 * BACK)]).astype(jnp.bfloat16)
        for index in range(8):
            rank = part * 8 + index
            head = (rank % 4) * PAIR_HEADS + rank // 4
            columns = pl.ds(head * HEAD_DIM, HEAD_DIM)
            first[:, columns] = rows[index * 16 : index * 16 + ROWS]
            second[:, columns] = rows[index * 16 + 8 : index * 16 + 8 + ROWS]


def finish(messages):
    shape = jax.ShapeDtypeStruct((ROWS, HEADS * HEAD_DIM), jnp.bfloat16)
    return pl.pallas_call(
        finish_kernel,
        out_shape=(shape, shape),
        compiler_params=pltpu.CompilerParams(vmem_limit_bytes=VMEM_LIMIT),
    )(messages)


def body(
    query_first,
    keys_first,
    values_first,
    query_second,
    keys_second,
    values_second,
    text_keys,
    text_values,
    gate_table,
    timesteps,
    text_length,
):
    sent, extra = pack(
        keys_first,
        values_first,
        query_first,
        query_second,
        keys_second,
        values_second,
        text_keys,
        text_values,
        gate_table,
        timesteps,
    )
    pairs = sent.reshape(PEERS, CHUNK // 2, 2, HEAD_DIM)
    arrived = lax.all_to_all(pairs, PLANE, 0, 0, tiled=True)
    copies, queries, near = unpack(arrived.reshape(PEERS * CHUNK, HEAD_DIM))
    planes = lax.all_to_all(copies, "x", 0, 0, tiled=True)
    mine = join(planes, near, extra)
    theirs = lax.ppermute(mine, "c", [(0, 1), (1, 0)])
    sums, tops = first_pass(queries, mine)
    back = second_pass(text_length, queries, mine, theirs, sums, tops)
    pairs = back.reshape(PEERS, ROWS, 2, HEAD_DIM)
    returned = lax.all_to_all(pairs, PLANE, 0, 0, tiled=True)
    return finish(returned.reshape(PEERS * BACK, HEAD_DIM))


def solution(mesh):
    fine = Mesh(mesh.devices.reshape(8, 4, 2, 4, 2), AXES)
    rows = P(AXES, None)
    heads = P(None, ("yh", "c"))
    return jax.shard_map(
        body,
        mesh=fine,
        in_specs=(rows,) * 6 + (heads,) * 3 + (P(), P()),
        out_specs=(rows, rows),
        check_vma=False,
    )
```

```python
import jax
import jax.numpy as jnp
import numpy as np
from jax import lax
from jax.experimental import pallas as pl
from jax.experimental.pallas import tpu as pltpu
from jax.sharding import Mesh
from jax.sharding import PartitionSpec as P

HEAD_DIM = 128
HEADS = 40
GROUP_HEADS = 5
PAIR_HEADS = 10
ROWS = 5
PLANE_ROWS = 320
BLOCK_ROWS = 20
PEERS = 64
CHUNK = 6 * ROWS
BACK = 2 * ROWS
TEXT = 512
EXP_SCALE = float(HEAD_DIM ** (-0.5) * np.log2(np.e))

AXES = ("z", "x", "yl", "yh", "c")
PLANE = ("z", "yl", "yh")
ACTIVE = 4 * PAIR_HEADS

EARLY_VALUES_AT = 2 * PLANE_ROWS
TEXT_AT = 2 * EARLY_VALUES_AT
EXTRA = 2 * TEXT + 16
EARLY = TEXT_AT + EXTRA
FAR = 3 * PLANE_ROWS
FAR_KEYS = 1024
LATE = FAR_KEYS + FAR

VMEM_LIMIT = 24 * 1024 * 1024


def dot_f32(left, right):
    return lax.dot_general(
        left, right, (((1,), (0,)), ((), ())), preferred_element_type=jnp.float32
    )


def dot_t_f32(left, right):
    return lax.dot_general(
        left, right, (((1,), (1,)), ((), ())), preferred_element_type=jnp.float32
    )


def head_slot():
    return lax.axis_index("z") * 2 + lax.axis_index("yl")


def in_hbm(array):
    return pltpu.with_memory_space_constraint(array, pltpu.HBM)


def one_hot(condition):
    return jnp.where(condition, 1.0, 0.0).astype(jnp.bfloat16)


def message_of(source, rows):
    return (source * (65536 // rows + 1)) // 65536


def pack_kernel(k1, v1, q1, q2, k2, v2, out, held, stacked, ready, fetch_sems, send_sems):
    fetches = [
        pltpu.make_async_copy(array, held.at[index], fetch_sems.at[index])
        for index, array in enumerate((k1, v1, q1, q2, k2, v2))
    ]
    for fetch in fetches:
        fetch.start()
    blank = pl.ds(ACTIVE * CHUNK, (PEERS - ACTIVE) * CHUNK)
    places = [pl.ds(part * 8 * CHUNK, 8 * CHUNK) for part in range(ACTIVE // 8)] + [blank]
    sends = [
        pltpu.make_async_copy(ready.at[place], out.at[place], send_sems.at[index])
        for index, place in enumerate(places)
    ]
    ready[blank] = jnp.zeros(((PEERS - ACTIVE) * CHUNK, HEAD_DIM), jnp.bfloat16)
    sends[-1].start()
    stacked[...] = jnp.zeros_like(stacked)
    for index in range(6):
        fetches[index].wait()
        stacked[pl.ds(index * 8, ROWS)] = held[index]
    source = lax.broadcasted_iota(jnp.int32, (1, 8 * 48), 1)
    message = message_of(source, 48)
    array = (source - message * 48) // 8
    entry = source - message * 48 - array * 8
    target = jnp.where(entry < ROWS, message * CHUNK + array * ROWS + entry, -1)
    order = one_hot(lax.broadcasted_iota(jnp.int32, (8 * CHUNK, 8 * 48), 0) == target)
    for part in range(ACTIVE // 8):
        pieces = []
        for rank in range(part * 8, part * 8 + 8):
            head = (rank % 4) * PAIR_HEADS + rank // 4
            pieces.append(stacked[:, head * HEAD_DIM : (head + 1) * HEAD_DIM])
        rows = dot_f32(order, jnp.concatenate(pieces, axis=0))
        ready[places[part]] = rows.astype(jnp.bfloat16)
        sends[part].start()
    for send in sends:
        send.wait()


def pack(*arrays):
    hbm = pl.BlockSpec(memory_space=pltpu.HBM)
    return pl.pallas_call(
        pack_kernel,
        out_shape=jax.ShapeDtypeStruct((PEERS * CHUNK, HEAD_DIM), jnp.bfloat16),
        in_specs=[hbm] * 6,
        out_specs=hbm,
        scratch_shapes=[
            pltpu.VMEM((6, ROWS, HEADS * HEAD_DIM), jnp.bfloat16),
            pltpu.VMEM((48, HEADS * HEAD_DIM), jnp.bfloat16),
            pltpu.VMEM((PEERS * CHUNK, HEAD_DIM), jnp.bfloat16),
            pltpu.SemaphoreType.DMA((6,)),
            pltpu.SemaphoreType.DMA((ACTIVE // 8 + 1,)),
        ],
        compiler_params=pltpu.CompilerParams(vmem_limit_bytes=VMEM_LIMIT),
    )(*[in_hbm(array) for array in arrays])


def prepare_kernel(length, steps, text_k, text_v, gates, extra, dead, order, gate, sems):
    slot = lax.rem(head_slot(), GROUP_HEADS)
    columns = pl.ds(pl.multiple_of(slot * HEAD_DIM, HEAD_DIM), HEAD_DIM)
    fetches = [
        pltpu.make_async_copy(text_k.at[:, columns], extra.at[pl.ds(0, TEXT)], sems.at[0]),
        pltpu.make_async_copy(text_v.at[:, columns], extra.at[pl.ds(TEXT, TEXT)], sems.at[1]),
        pltpu.make_async_copy(gates.at[:, columns], gate, sems.at[2]),
    ]
    for fetch in fetches:
        fetch.start()
    source = lax.broadcasted_iota(jnp.int32, (1, 8 * CHUNK), 1)
    message = message_of(source, CHUNK)
    entry = source - message * CHUNK
    target = entry + ((entry * 13) // 64) * 35 + message * ROWS
    order[...] = one_hot(lax.broadcasted_iota(jnp.int32, (240, 8 * CHUNK), 0) == target)
    slots = lax.broadcasted_iota(jnp.int32, (8, TEXT), 1)
    dead[...] = jnp.where(slots < length[0], 0.0, 1.0)
    for fetch in fetches:
        fetch.wait()
    row = lax.broadcasted_iota(jnp.int32, (16, HEAD_DIM), 0)
    parts = jnp.zeros((16, HEAD_DIM), jnp.float32)
    for step in range(2):
        left = gate[pl.ds(steps[step], 1), :]
        for index in range(3):
            part = left.astype(jnp.bfloat16).astype(jnp.float32)
            parts = jnp.where(row == step * 3 + index, part, parts)
            left = left - part
    extra[pl.ds(2 * TEXT, 16)] = parts.astype(jnp.bfloat16)


def prepare(text_length, timesteps, text_keys, text_values, gate_table):
    smem = pl.BlockSpec(memory_space=pltpu.SMEM)
    hbm = pl.BlockSpec(memory_space=pltpu.HBM)
    vmem = pl.BlockSpec(memory_space=pltpu.VMEM)
    return pl.pallas_call(
        prepare_kernel,
        out_shape=(
            jax.ShapeDtypeStruct((EXTRA, HEAD_DIM), jnp.bfloat16),
            jax.ShapeDtypeStruct((8, TEXT), jnp.float32),
            jax.ShapeDtypeStruct((240, 8 * CHUNK), jnp.bfloat16),
        ),
        in_specs=[smem, smem, hbm, hbm, hbm],
        out_specs=(vmem, vmem, vmem),
        scratch_shapes=[
            pltpu.VMEM((35, HEAD_DIM), jnp.float32),
            pltpu.SemaphoreType.DMA((3,)),
        ],
        compiler_params=pltpu.CompilerParams(vmem_limit_bytes=VMEM_LIMIT),
    )(text_length, timesteps, in_hbm(text_keys), in_hbm(text_values), in_hbm(gate_table))


def unpack_kernel(messages, extra, order, copies, queries, early, plane, sems):
    def ordered(step, first, last):
        rows = messages[pl.ds(step * 8 * CHUNK, 8 * CHUNK)]
        result = dot_f32(order[pl.ds(first * 40, (last - first) * 40)], rows)
        return result.astype(jnp.bfloat16)

    for step in range(8):
        result = ordered(step, 0, 2)
        for array in range(2):
            piece = result[array * 40 : (array + 1) * 40]
            plane[pl.ds(array * PLANE_ROWS + step * 40, 40)] = piece
            early[pl.ds(array * EARLY_VALUES_AT + step * 40, 40)] = piece
    sends = [pltpu.make_async_copy(plane, copies.at[copy], sems.at[copy]) for copy in range(4)]
    for send in sends:
        send.start()
    for step in range(8):
        result = ordered(step, 2, 6)
        for array in range(4):
            piece = result[array * 40 : (array + 1) * 40]
            if array < 2:
                queries[pl.ds(array * PLANE_ROWS + step * 40, 40)] = piece
            else:
                begin = (array - 2) * EARLY_VALUES_AT + PLANE_ROWS
                early[pl.ds(begin + step * 40, 40)] = piece
    early[pl.ds(TEXT_AT, EXTRA)] = extra[...]
    for send in sends:
        send.wait()


def unpack(messages, extra, order):
    vmem = pl.BlockSpec(memory_space=pltpu.VMEM)
    return pl.pallas_call(
        unpack_kernel,
        out_shape=(
            jax.ShapeDtypeStruct((4, 2 * PLANE_ROWS, HEAD_DIM), jnp.bfloat16),
            jax.ShapeDtypeStruct((2 * PLANE_ROWS, HEAD_DIM), jnp.bfloat16),
            jax.ShapeDtypeStruct((EARLY, HEAD_DIM), jnp.bfloat16),
        ),
        in_specs=[vmem] * 3,
        out_specs=(pl.BlockSpec(memory_space=pltpu.HBM), vmem, vmem),
        scratch_shapes=[
            pltpu.VMEM((2 * PLANE_ROWS, HEAD_DIM), jnp.bfloat16),
            pltpu.SemaphoreType.DMA((4,)),
        ],
        compiler_params=pltpu.CompilerParams(vmem_limit_bytes=VMEM_LIMIT),
    )(messages, extra, order)


def join_kernel(planes, behind, out):
    del behind
    own = lax.axis_index("x")
    for place in range(3):
        source = lax.rem(own + place + 1, 4)
        for part in range(2):
            out[pl.ds(part * FAR_KEYS + place * PLANE_ROWS, PLANE_ROWS)] = planes[
                source, pl.ds(part * PLANE_ROWS, PLANE_ROWS)
            ]
    out[pl.ds(FAR, FAR_KEYS - FAR)] = planes[lax.rem(own + 1, 4), pl.ds(0, FAR_KEYS - FAR)]


def join(planes, behind):
    return pl.pallas_call(
        join_kernel,
        out_shape=jax.ShapeDtypeStruct((LATE, HEAD_DIM), jnp.bfloat16),
        compiler_params=pltpu.CompilerParams(vmem_limit_bytes=VMEM_LIMIT),
    )(planes, behind)


TILE = 160
TILES = 2 * PLANE_ROWS // TILE


def block_of(index):
    return jnp.floor((index.astype(jnp.float32) + 0.5) * (1.0 / BLOCK_ROWS))


def beside_ones(target, rows):
    target[:, :HEAD_DIM] = rows
    target[:, HEAD_DIM:] = jnp.ones_like(rows)


def tile_rows(tile):
    return pl.ds(tile * TILE, TILE)


class OwnPart:
    def __init__(self, queries, early, values):
        self.queries, self.early, self.values = queries, early, values
        beside_ones(values, early[pl.ds(EARLY_VALUES_AT, 2 * PLANE_ROWS)])

    def width(self, tile):
        return 384 if tile * TILE < PLANE_ROWS else 2 * PLANE_ROWS

    def scores(self, tile):
        width = self.width(tile)
        scores = dot_t_f32(self.queries[tile_rows(tile)], self.early[pl.ds(0, width)])
        column = lax.broadcasted_iota(jnp.int32, (1, width), 1)
        first = column < PLANE_ROWS
        if tile * TILE < PLANE_ROWS:
            return jnp.where(first, scores, -1e30)
        row = lax.broadcasted_iota(jnp.int32, (TILE, 1), 0) + (tile * TILE) % PLANE_ROWS
        same = block_of(row) == block_of(jnp.where(first, column, column - PLANE_ROWS))
        return jnp.where(jnp.logical_xor(same, first), scores, -1e30)

    def sums(self, weights, tile):
        return dot_f32(weights, self.values[pl.ds(0, self.width(tile))])


class TextPart:
    def __init__(self, queries, dead, text, values):
        self.queries, self.dead, self.text, self.values = queries, dead, text, values
        beside_ones(values, text[pl.ds(TEXT, TEXT)])

    def scores(self, tile):
        scores = dot_t_f32(self.queries[tile_rows(tile)], self.text[pl.ds(0, TEXT)])
        return jnp.where(self.dead[0:1] == 0.0, scores, -1e30)

    def sums(self, weights, tile):
        return dot_f32(weights, self.values[...])


class FarPart:
    def __init__(self, queries, late, values, half):
        self.queries, self.late, self.values = queries, late, values
        self.place = pl.ds(half * (FAR_KEYS // 2), FAR_KEYS // 2)
        if half == 0:
            beside_ones(values.at[pl.ds(0, FAR)], late[pl.ds(FAR_KEYS, FAR)])
            rest = FAR_KEYS - FAR
            values[pl.ds(FAR, rest)] = jnp.zeros((rest, 2 * HEAD_DIM), jnp.bfloat16)

    def scores(self, tile):
        return dot_t_f32(self.queries[tile_rows(tile)], self.late[self.place])

    def sums(self, weights, tile):
        return dot_f32(weights, self.values[self.place])


def lane_max(scores, former):
    for begin in range(0, scores.shape[1], HEAD_DIM):
        piece = scores[:, begin : begin + HEAD_DIM]
        former = piece if former is None else jnp.maximum(former, piece)
    return former


def weigh(scores, top):
    return jnp.exp2((scores - top) * EXP_SCALE).astype(jnp.bfloat16)


def run_tiles(parts, before, finish_tile):
    former = None
    for tile in range(TILES + 1):
        scores, lanes, sums = [], None, None
        for index, part in enumerate(parts):
            if tile < TILES:
                scores.append(part.scores(tile))
                lanes = lane_max(scores[-1], lanes)
            if former is not None:
                fresh = part.sums(weigh(former[0][index], former[1]), tile - 1)
                sums = fresh if sums is None else sums + fresh
        if former is not None:
            top = former[1]
            if before is not None:
                scale = jnp.exp2((before[1][tile_rows(tile - 1), 0:1] - top) * EXP_SCALE)
                sums = sums + before[0][tile_rows(tile - 1)] * scale
            finish_tile(tile - 1, top, sums)
        if tile < TILES:
            top = jnp.max(lanes, axis=1, keepdims=True)
            if before is not None:
                top = jnp.maximum(before[1][tile_rows(tile), 0:1], top)
            former = (scores, top)


def keep(sums, tops):
    def finish_tile(tile, top, total):
        sums[tile_rows(tile)] = total
        tops[tile_rows(tile)] = jnp.broadcast_to(top, (TILE, HEAD_DIM))

    return finish_tile


STATE = (
    jax.ShapeDtypeStruct((2 * PLANE_ROWS, 2 * HEAD_DIM), jnp.float32),
    jax.ShapeDtypeStruct((2 * PLANE_ROWS, HEAD_DIM), jnp.float32),
)


def values_scratch(rows):
    return pltpu.VMEM((rows, 2 * HEAD_DIM), jnp.bfloat16)


def mine_kernel(queries, early, sums, tops, values):
    run_tiles([OwnPart(queries, early, values)], None, keep(sums, tops))


def mine_pass(queries, early):
    return pl.pallas_call(
        mine_kernel,
        out_shape=STATE,
        scratch_shapes=[values_scratch(2 * PLANE_ROWS)],
        cost_estimate=pl.CostEstimate(flops=8 * 10**9, bytes_accessed=0, transcendentals=0),
        compiler_params=pltpu.CompilerParams(vmem_limit_bytes=VMEM_LIMIT),
    )(queries, early)


def theirs_kernel(
    dead, queries, mine, theirs, sums, tops, new_sums, new_tops, gate, values, text, text_values
):
    here = head_slot() // GROUP_HEADS == lax.axis_index("c")

    @pl.when(here)
    def _():
        text[...] = mine[pl.ds(TEXT_AT, EXTRA)]

    @pl.when(jnp.logical_not(here))
    def _():
        text[...] = theirs[pl.ds(TEXT_AT, EXTRA)]

    parts = text[pl.ds(2 * TEXT, 16)].astype(jnp.float32)
    for step in range(2):
        row = parts[3 * step : 3 * step + 1] + parts[3 * step + 1 : 3 * step + 2]
        gate[pl.ds(step, 1)] = row + parts[3 * step + 2 : 3 * step + 3]
    run_tiles(
        [OwnPart(queries, theirs, values), TextPart(queries, dead, text, text_values)],
        (sums, tops),
        keep(new_sums, new_tops),
    )


def theirs_pass(dead, queries, mine, theirs, sums, tops):
    vmem = pl.BlockSpec(memory_space=pltpu.VMEM)
    return pl.pallas_call(
        theirs_kernel,
        out_shape=STATE + (jax.ShapeDtypeStruct((2, HEAD_DIM), jnp.float32),),
        in_specs=[vmem] * 6,
        out_specs=(vmem, vmem, vmem),
        scratch_shapes=[
            values_scratch(2 * PLANE_ROWS),
            pltpu.VMEM((EXTRA, HEAD_DIM), jnp.bfloat16),
            values_scratch(TEXT),
        ],
        compiler_params=pltpu.CompilerParams(vmem_limit_bytes=VMEM_LIMIT),
    )(dead, queries, mine, theirs, sums, tops)


def far_parts(queries, late, values):
    return [FarPart(queries, late, values, half) for half in range(2)]


def far_kernel(queries, late, sums, tops, new_sums, new_tops, values):
    run_tiles(far_parts(queries, late, values), (sums, tops), keep(new_sums, new_tops))


def far_pass(queries, late, sums, tops):
    return pl.pallas_call(
        far_kernel,
        out_shape=STATE,
        scratch_shapes=[values_scratch(FAR_KEYS)],
        compiler_params=pltpu.CompilerParams(vmem_limit_bytes=VMEM_LIMIT),
    )(queries, late, sums, tops)


def last_kernel(queries, late, sums, tops, gate, out, values, done):
    def finish_tile(tile, top, total):
        step = tile * TILE // PLANE_ROWS
        attended = total[:, :HEAD_DIM] / total[:, HEAD_DIM:]
        done[tile_rows(tile)] = (gate[pl.ds(step, 1)] * attended).astype(jnp.bfloat16)

    run_tiles(far_parts(queries, late, values), (sums, tops), finish_tile)
    row = lax.broadcasted_iota(jnp.int32, (160, 80), 0)
    column = lax.broadcasted_iota(jnp.int32, (160, 80), 1)
    place_first = one_hot(row == 2 * column)
    place_second = one_hot(row == 2 * column + 1)
    for part in range(4):
        rows = dot_f32(place_first, done[pl.ds(part * 80, 80)])
        rows += dot_f32(place_second, done[pl.ds(PLANE_ROWS + part * 80, 80)])
        out[pl.ds(part * 160, 160)] = rows.astype(jnp.bfloat16)


def last_pass(queries, late, sums, tops, gate):
    return pl.pallas_call(
        last_kernel,
        out_shape=jax.ShapeDtypeStruct((PEERS * BACK, HEAD_DIM), jnp.bfloat16),
        scratch_shapes=[
            values_scratch(FAR_KEYS),
            pltpu.VMEM((2 * PLANE_ROWS, HEAD_DIM), jnp.bfloat16),
        ],
        compiler_params=pltpu.CompilerParams(vmem_limit_bytes=VMEM_LIMIT),
    )(queries, late, sums, tops, gate)


def finish_kernel(messages, first, second):
    source = lax.broadcasted_iota(jnp.int32, (1, 8 * BACK), 1)
    message = message_of(source, BACK)
    entry = source - message * BACK
    target = message * 16 + (entry % 2) * 8 + entry // 2
    order = one_hot(lax.broadcasted_iota(jnp.int32, (128, 8 * BACK), 0) == target)
    for part in range(ACTIVE // 8):
        rows = dot_f32(order, messages[pl.ds(part * 8 * BACK, 8 * BACK)]).astype(jnp.bfloat16)
        for index in range(8):
            rank = part * 8 + index
            head = (rank % 4) * PAIR_HEADS + rank // 4
            columns = pl.ds(head * HEAD_DIM, HEAD_DIM)
            first[:, columns] = rows[index * 16 : index * 16 + ROWS]
            second[:, columns] = rows[index * 16 + 8 : index * 16 + 8 + ROWS]


def finish(messages):
    shape = jax.ShapeDtypeStruct((ROWS, HEADS * HEAD_DIM), jnp.bfloat16)
    return pl.pallas_call(
        finish_kernel,
        out_shape=(shape, shape),
        compiler_params=pltpu.CompilerParams(vmem_limit_bytes=VMEM_LIMIT),
    )(messages)


def body(
    query_first,
    keys_first,
    values_first,
    query_second,
    keys_second,
    values_second,
    text_keys,
    text_values,
    gate_table,
    timesteps,
    text_length,
):
    sent = pack(keys_first, values_first, query_first, query_second, keys_second, values_second)
    pairs = sent.reshape(PEERS, CHUNK // 2, 2, HEAD_DIM)
    arrived = lax.all_to_all(pairs, PLANE, 0, 0, tiled=True)
    extra, dead, order = prepare(text_length, timesteps, text_keys, text_values, gate_table)
    copies, queries, mine = unpack(arrived.reshape(PEERS * CHUNK, HEAD_DIM), extra, order)
    planes = lax.all_to_all(copies, "x", 0, 0, tiled=True)
    theirs = lax.ppermute(mine, "c", [(0, 1), (1, 0)])
    sums, tops = mine_pass(queries, mine)
    sums, tops, gate = theirs_pass(dead, queries, mine, theirs, sums, tops)
    late_mine = join(planes, gate)
    late_theirs = lax.ppermute(late_mine, "c", [(0, 1), (1, 0)])
    sums, tops = far_pass(queries, late_mine, sums, tops)
    back = last_pass(queries, late_theirs, sums, tops, gate)
    pairs = back.reshape(PEERS, ROWS, 2, HEAD_DIM)
    returned = lax.all_to_all(pairs, PLANE, 0, 0, tiled=True)
    return finish(returned.reshape(PEERS * BACK, HEAD_DIM))


def solution(mesh):
    fine = Mesh(mesh.devices.reshape(8, 4, 2, 4, 2), AXES)
    rows = P(AXES, None)
    heads = P(None, ("yh", "c"))
    return jax.shard_map(
        body,
        mesh=fine,
        in_specs=(rows,) * 6 + (heads,) * 3 + (P(), P()),
        out_specs=(rows, rows),
        check_vma=False,
    )
```

```python
import jax
import jax.numpy as jnp
import numpy as np
from jax import lax
from jax.experimental import pallas as pl
from jax.experimental.pallas import tpu as pltpu
from jax.sharding import Mesh
from jax.sharding import PartitionSpec as P

HEAD_DIM = 128
HEADS = 40
GROUP_HEADS = 5
PAIR_HEADS = 10
ROWS = 5
PLANE_ROWS = 320
PEERS = 64
CHUNK = 6 * ROWS
BACK = 2 * ROWS
TEXT = 512
EXP_SCALE = float(HEAD_DIM ** (-0.5) * np.log2(np.e))

AXES = ("z", "x", "yl", "yh", "c")
PLANE = ("z", "yh", "yl")
ACTIVE = 4 * PAIR_HEADS

HALF = 4 * PLANE_ROWS
NEAR_AT = 2 * HALF
TEXT_AT = NEAR_AT + 2 * PLANE_ROWS
GATE_AT = TEXT_AT + 2 * TEXT
SHARED = GATE_AT + 16
EXTRA = SHARED - TEXT_AT

VMEM_LIMIT = 48 * 1024 * 1024


def dot_f32(left, right):
    return lax.dot_general(
        left, right, (((1,), (0,)), ((), ())), preferred_element_type=jnp.float32
    )


def dot_t_f32(left, right):
    return lax.dot_general(
        left, right, (((1,), (1,)), ((), ())), preferred_element_type=jnp.float32
    )


def head_slot():
    return lax.axis_index("z") * 2 + lax.axis_index("yl")


def head_of(rank):
    return (rank % 8) // 2 * PAIR_HEADS + rank // 8 * 2 + rank % 2


def in_hbm(array):
    return pltpu.with_memory_space_constraint(array, pltpu.HBM)


def one_hot(condition):
    return jnp.where(condition, 1.0, 0.0).astype(jnp.bfloat16)


def message_of(source, rows):
    return (source * (65536 // rows + 1)) // 65536


def pack_kernel(
    k1, v1, q1, q2, k2, v2, text_k, text_v, gates, steps, out, extra,
    held, stacked, gate, step_ids, sems,
):
    slot = lax.rem(head_slot(), GROUP_HEADS)
    columns = pl.ds(pl.multiple_of(slot * HEAD_DIM, HEAD_DIM), HEAD_DIM)
    targets = [(array, held.at[index]) for index, array in enumerate((k1, v1, q1, q2, k2, v2))]
    targets += [
        (steps, step_ids),
        (gates.at[:, columns], gate),
        (text_k.at[:, columns], extra.at[pl.ds(0, TEXT)]),
        (text_v.at[:, columns], extra.at[pl.ds(TEXT, TEXT)]),
    ]
    fetches = [
        pltpu.make_async_copy(source, target, sems.at[index])
        for index, (source, target) in enumerate(targets)
    ]
    for fetch in fetches:
        fetch.start()
    stacked[...] = jnp.zeros_like(stacked)
    source = lax.broadcasted_iota(jnp.int32, (1, 8 * 48), 1)
    message = message_of(source, 48)
    array = (source - message * 48) // 8
    entry = source - message * 48 - array * 8
    target = jnp.where(entry < ROWS, message * CHUNK + array * ROWS + entry, -1)
    order = one_hot(lax.broadcasted_iota(jnp.int32, (8 * CHUNK, 8 * 48), 0) == target)
    for index in range(6):
        fetches[index].wait()
        stacked[pl.ds(index * 8, ROWS)] = held[index]
    for part in range(PEERS // 8):
        place = pl.ds(part * 8 * CHUNK, 8 * CHUNK)
        if part * 8 >= ACTIVE:
            out[place] = jnp.zeros((8 * CHUNK, HEAD_DIM), jnp.bfloat16)
            continue
        pieces = []
        for rank in range(part * 8, part * 8 + 8):
            head = head_of(rank)
            pieces.append(stacked[:, head * HEAD_DIM : (head + 1) * HEAD_DIM])
        out[place] = dot_f32(order, jnp.concatenate(pieces, axis=0)).astype(jnp.bfloat16)
    for fetch in fetches[6:]:
        fetch.wait()
    row = lax.broadcasted_iota(jnp.int32, (16, HEAD_DIM), 0)
    parts = jnp.zeros((16, HEAD_DIM), jnp.float32)
    for step in range(2):
        left = gate[pl.ds(step_ids[step], 1), :]
        for index in range(3):
            part = left.astype(jnp.bfloat16).astype(jnp.float32)
            parts = jnp.where(row == step * 3 + index, part, parts)
            left = left - part
    extra[pl.ds(2 * TEXT, 16)] = parts.astype(jnp.bfloat16)


def pack(*arrays):
    vmem = pl.BlockSpec(memory_space=pltpu.VMEM)
    return pl.pallas_call(
        pack_kernel,
        out_shape=(
            jax.ShapeDtypeStruct((PEERS * CHUNK, HEAD_DIM), jnp.bfloat16),
            jax.ShapeDtypeStruct((EXTRA, HEAD_DIM), jnp.bfloat16),
        ),
        in_specs=[pl.BlockSpec(memory_space=pltpu.HBM)] * 10,
        out_specs=(vmem, vmem),
        scratch_shapes=[
            pltpu.VMEM((6, ROWS, HEADS * HEAD_DIM), jnp.bfloat16),
            pltpu.VMEM((48, HEADS * HEAD_DIM), jnp.bfloat16),
            pltpu.VMEM((35, HEAD_DIM), jnp.float32),
            pltpu.SMEM((2,), jnp.int32),
            pltpu.SemaphoreType.DMA((10,)),
        ],
        compiler_params=pltpu.CompilerParams(vmem_limit_bytes=VMEM_LIMIT),
    )(*[in_hbm(array) for array in arrays])


def unpack_kernel(messages, copies, queries, near):
    source = lax.broadcasted_iota(jnp.int32, (1, 8 * CHUNK), 1)
    message = message_of(source, CHUNK)
    entry = source - message * CHUNK
    target = entry + ((entry * 13) // 64) * 35 + message * ROWS
    order = one_hot(lax.broadcasted_iota(jnp.int32, (240, 8 * CHUNK), 0) == target)
    for step in range(8):
        rows = messages[pl.ds(step * 8 * CHUNK, 8 * CHUNK)]
        ordered = dot_f32(order, rows).astype(jnp.bfloat16)
        for array in range(6):
            piece = ordered[array * 40 : (array + 1) * 40]
            place = pl.ds((array % 2) * PLANE_ROWS + step * 40, 40)
            if array < 2:
                for copy in range(4):
                    copies[copy, place] = piece
            elif array < 4:
                queries[place] = piece
            else:
                near[place] = piece


def unpack(messages):
    rows = jax.ShapeDtypeStruct((2 * PLANE_ROWS, HEAD_DIM), jnp.bfloat16)
    return pl.pallas_call(
        unpack_kernel,
        out_shape=(
            jax.ShapeDtypeStruct((4, 2 * PLANE_ROWS, HEAD_DIM), jnp.bfloat16),
            rows,
            rows,
        ),
        compiler_params=pltpu.CompilerParams(vmem_limit_bytes=VMEM_LIMIT),
    )(messages)


def join_kernel(planes, near, extra, out):
    own = lax.axis_index("x")
    for place in range(4):
        source = lax.rem(own + place, 4)
        for part in range(2):
            out[pl.ds(part * HALF + place * PLANE_ROWS, PLANE_ROWS)] = planes[
                source, pl.ds(part * PLANE_ROWS, PLANE_ROWS)
            ]
    out[pl.ds(NEAR_AT, 2 * PLANE_ROWS)] = near[...]
    out[pl.ds(TEXT_AT, EXTRA)] = extra[...]


def join(planes, near, extra):
    return pl.pallas_call(
        join_kernel,
        out_shape=jax.ShapeDtypeStruct((SHARED, HEAD_DIM), jnp.bfloat16),
        compiler_params=pltpu.CompilerParams(vmem_limit_bytes=VMEM_LIMIT),
    )(planes, near, extra)


TILE = 160
TILES = 2 * PLANE_ROWS // TILE
NEAR = 384
CUTS = ((0, 512), (512, 1024), (1024, HALF))


def floor_of(index, step):
    return jnp.floor((index + 0.5) * (1.0 / step))


def block_of(index):
    message = floor_of(index.astype(jnp.float32), ROWS)
    return 2.0 * floor_of(message, 8) + message - 2.0 * floor_of(message, 2)


def beside_ones(target, rows):
    target[:, :HEAD_DIM] = rows
    target[:, HEAD_DIM:] = jnp.ones_like(rows)


def same_block(tile):
    row = lax.broadcasted_iota(jnp.int32, (TILE, 1), 0) + (tile * TILE) % PLANE_ROWS
    column = lax.broadcasted_iota(jnp.int32, (1, NEAR), 1)
    return block_of(row) == block_of(column)


def tile_rows(tile):
    return pl.ds(tile * TILE, TILE)


def half_scores(queries, keys, tile, cut):
    rows = queries[tile_rows(tile)]
    scores = dot_t_f32(rows, keys[pl.ds(cut[0], cut[1] - cut[0])])
    if tile * TILE >= PLANE_ROWS and cut[0] == 0:
        near = dot_t_f32(rows, keys[pl.ds(NEAR_AT, NEAR)])
        near = jnp.where(same_block(tile), near, scores[:, :NEAR])
        scores = jnp.concatenate([near, scores[:, NEAR:]], axis=1)
    return scores


def half_sums(weights, values, near_values, tile, cut):
    part = values[pl.ds(cut[0], cut[1] - cut[0])]
    if tile * TILE >= PLANE_ROWS and cut[0] == 0:
        same = same_block(tile)
        local = weights[:, :NEAR]
        blank = jnp.zeros_like(local)
        far = jnp.concatenate([jnp.where(same, blank, local), weights[:, NEAR:]], axis=1)
        return dot_f32(far, part) + dot_f32(jnp.where(same, local, blank), near_values[...])
    return dot_f32(weights, part)


def lane_max(scores, former):
    for begin in range(0, scores.shape[1], HEAD_DIM):
        piece = scores[:, begin : begin + HEAD_DIM]
        former = piece if former is None else jnp.maximum(former, piece)
    return former


def weigh(scores, top):
    return jnp.exp2((scores - top) * EXP_SCALE).astype(jnp.bfloat16)


def run_tiles(score_parts, sum_parts, start_top, finish_tile):
    former = None
    for tile in range(TILES + 1):
        scores, lanes, sums = [], None, None
        for index in range(len(score_parts)):
            if tile < TILES:
                part = score_parts[index](tile)
                lanes = lane_max(part, lanes)
                scores.append(part)
            if former is not None:
                part = sum_parts[index](weigh(former[0][index], former[1]), tile - 1)
                sums = part if sums is None else sums + part
        if former is not None:
            finish_tile(tile - 1, former[1], sums)
        if tile < TILES:
            top = jnp.max(lanes, axis=1, keepdims=True)
            former = (scores, start_top(tile, top))


def first_kernel(queries, mine, sums, tops, values, near_values):
    beside_ones(values, mine[pl.ds(HALF, HALF)])
    beside_ones(near_values, mine[pl.ds(NEAR_AT + PLANE_ROWS, NEAR)])

    def finish_tile(tile, top, total):
        sums[tile_rows(tile)] = total
        tops[tile_rows(tile)] = jnp.broadcast_to(top, (TILE, HEAD_DIM))

    run_tiles(
        [lambda tile, cut=cut: half_scores(queries, mine, tile, cut) for cut in CUTS],
        [
            lambda weights, tile, cut=cut: half_sums(weights, values, near_values, tile, cut)
            for cut in CUTS
        ],
        lambda tile, top: top,
        finish_tile,
    )


def second_kernel(
    length, queries, mine, theirs, sums, tops, out, values, near_values, text, text_values, done
):
    here = head_slot() // GROUP_HEADS == lax.axis_index("c")

    @pl.when(here)
    def _():
        text[...] = mine[pl.ds(TEXT_AT, EXTRA)]

    @pl.when(jnp.logical_not(here))
    def _():
        text[...] = theirs[pl.ds(TEXT_AT, EXTRA)]

    beside_ones(values, theirs[pl.ds(HALF, HALF)])
    beside_ones(near_values, theirs[pl.ds(NEAR_AT + PLANE_ROWS, NEAR)])
    beside_ones(text_values, text[pl.ds(TEXT, TEXT)])
    parts = text[pl.ds(2 * TEXT, 16)].astype(jnp.float32)
    live = lax.broadcasted_iota(jnp.int32, (1, TEXT), 1) < length[0]

    def text_scores(tile):
        scores = dot_t_f32(queries[tile_rows(tile)], text[pl.ds(0, TEXT)])
        return jnp.where(live, scores, -1e30)

    def start_top(tile, top):
        return jnp.maximum(tops[tile_rows(tile), 0:1], top)

    def finish_tile(tile, top, total):
        former = jnp.exp2((tops[tile_rows(tile), 0:1] - top) * EXP_SCALE)
        total = total + sums[tile_rows(tile)] * former
        step = tile * TILE // PLANE_ROWS
        gate = parts[3 * step : 3 * step + 1] + parts[3 * step + 1 : 3 * step + 2]
        gate = gate + parts[3 * step + 2 : 3 * step + 3]
        attended = total[:, :HEAD_DIM] / total[:, HEAD_DIM:]
        done[tile_rows(tile)] = (gate * attended).astype(jnp.bfloat16)

    run_tiles(
        [lambda tile, cut=cut: half_scores(queries, theirs, tile, cut) for cut in CUTS]
        + [text_scores],
        [
            lambda weights, tile, cut=cut: half_sums(weights, values, near_values, tile, cut)
            for cut in CUTS
        ]
        + [lambda weights, tile: dot_f32(weights, text_values[...])],
        start_top,
        finish_tile,
    )
    row = lax.broadcasted_iota(jnp.int32, (160, 80), 0)
    column = lax.broadcasted_iota(jnp.int32, (160, 80), 1)
    place_first = one_hot(row == 2 * column)
    place_second = one_hot(row == 2 * column + 1)
    for part in range(4):
        rows = dot_f32(place_first, done[pl.ds(part * 80, 80)])
        rows += dot_f32(place_second, done[pl.ds(PLANE_ROWS + part * 80, 80)])
        out[pl.ds(part * 160, 160)] = rows.astype(jnp.bfloat16)


def first_pass(queries, mine):
    vmem = pl.BlockSpec(memory_space=pltpu.VMEM)
    return pl.pallas_call(
        first_kernel,
        out_shape=(
            jax.ShapeDtypeStruct((2 * PLANE_ROWS, 2 * HEAD_DIM), jnp.float32),
            jax.ShapeDtypeStruct((2 * PLANE_ROWS, HEAD_DIM), jnp.float32),
        ),
        in_specs=[vmem, vmem],
        out_specs=(vmem, vmem),
        scratch_shapes=[
            pltpu.VMEM((HALF, 2 * HEAD_DIM), jnp.bfloat16),
            pltpu.VMEM((NEAR, 2 * HEAD_DIM), jnp.bfloat16),
        ],
        cost_estimate=pl.CostEstimate(
            flops=4 * 640 * 1600 * HEAD_DIM, bytes_accessed=2 * SHARED * HEAD_DIM, transcendentals=640 * HALF
        ),
        compiler_params=pltpu.CompilerParams(vmem_limit_bytes=VMEM_LIMIT),
    )(queries, mine)


def second_pass(text_length, queries, mine, theirs, sums, tops):
    vmem = pl.BlockSpec(memory_space=pltpu.VMEM)
    return pl.pallas_call(
        second_kernel,
        out_shape=jax.ShapeDtypeStruct((PEERS * BACK, HEAD_DIM), jnp.bfloat16),
        in_specs=[pl.BlockSpec(memory_space=pltpu.SMEM)] + [vmem] * 5,
        out_specs=vmem,
        scratch_shapes=[
            pltpu.VMEM((HALF, 2 * HEAD_DIM), jnp.bfloat16),
            pltpu.VMEM((NEAR, 2 * HEAD_DIM), jnp.bfloat16),
            pltpu.VMEM((EXTRA, HEAD_DIM), jnp.bfloat16),
            pltpu.VMEM((TEXT, 2 * HEAD_DIM), jnp.bfloat16),
            pltpu.VMEM((2 * PLANE_ROWS, HEAD_DIM), jnp.bfloat16),
        ],
        compiler_params=pltpu.CompilerParams(vmem_limit_bytes=VMEM_LIMIT),
    )(text_length, queries, mine, theirs, sums, tops)


def finish_kernel(messages, first, second):
    source = lax.broadcasted_iota(jnp.int32, (1, 8 * BACK), 1)
    message = message_of(source, BACK)
    entry = source - message * BACK
    target = message * 16 + (entry % 2) * 8 + entry // 2
    order = one_hot(lax.broadcasted_iota(jnp.int32, (128, 8 * BACK), 0) == target)
    for part in range(ACTIVE // 8):
        rows = dot_f32(order, messages[pl.ds(part * 8 * BACK, 8 * BACK)]).astype(jnp.bfloat16)
        for index in range(8):
            rank = part * 8 + index
            head = head_of(rank)
            columns = pl.ds(head * HEAD_DIM, HEAD_DIM)
            first[:, columns] = rows[index * 16 : index * 16 + ROWS]
            second[:, columns] = rows[index * 16 + 8 : index * 16 + 8 + ROWS]


def finish(messages):
    shape = jax.ShapeDtypeStruct((ROWS, HEADS * HEAD_DIM), jnp.bfloat16)
    return pl.pallas_call(
        finish_kernel,
        out_shape=(shape, shape),
        compiler_params=pltpu.CompilerParams(vmem_limit_bytes=VMEM_LIMIT),
    )(messages)


def body(
    query_first,
    keys_first,
    values_first,
    query_second,
    keys_second,
    values_second,
    text_keys,
    text_values,
    gate_table,
    timesteps,
    text_length,
):
    sent, extra = pack(
        keys_first,
        values_first,
        query_first,
        query_second,
        keys_second,
        values_second,
        text_keys,
        text_values,
        gate_table,
        timesteps,
    )
    pairs = sent.reshape(PEERS, CHUNK // 2, 2, HEAD_DIM)
    arrived = lax.all_to_all(pairs, PLANE, 0, 0, tiled=True)
    copies, queries, near = unpack(arrived.reshape(PEERS * CHUNK, HEAD_DIM))
    planes = lax.all_to_all(copies, "x", 0, 0, tiled=True)
    mine = join(planes, near, extra)
    theirs = lax.ppermute(mine, "c", [(0, 1), (1, 0)])
    sums, tops = first_pass(queries, mine)
    back = second_pass(text_length, queries, mine, theirs, sums, tops)
    pairs = back.reshape(PEERS, ROWS, 2, HEAD_DIM)
    returned = lax.all_to_all(pairs, PLANE, 0, 0, tiled=True)
    return finish(returned.reshape(PEERS * BACK, HEAD_DIM))


def solution(mesh):
    fine = Mesh(mesh.devices.reshape(8, 4, 2, 4, 2), AXES)
    rows = P(AXES, None)
    heads = P(None, ("yh", "c"))
    return jax.shard_map(
        body,
        mesh=fine,
        in_specs=(rows,) * 6 + (heads,) * 3 + (P(), P()),
        out_specs=(rows, rows),
        check_vma=False,
    )
```

```python
import jax
import jax.numpy as jnp
import numpy as np
from jax import lax
from jax.experimental import pallas as pl
from jax.experimental.pallas import tpu as pltpu
from jax.sharding import Mesh
from jax.sharding import PartitionSpec as P

HEAD_DIM = 128
HEADS = 40
GROUP_HEADS = 5
PAIR_HEADS = 10
ROWS = 5
PLANE_ROWS = 320
PEERS = 64
CHUNK = 6 * ROWS
BACK = 2 * ROWS
TEXT = 512
EXP_SCALE = float(HEAD_DIM ** (-0.5) * np.log2(np.e))

AXES = ("z", "x", "yl", "yh", "c")
PLANE = ("yh", "z", "yl")

HALF = 4 * PLANE_ROWS
NEAR_AT = 2 * HALF
TEXT_AT = NEAR_AT + 2 * PLANE_ROWS
GATE_AT = TEXT_AT + 2 * TEXT
SHARED = GATE_AT + 16
EXTRA = SHARED - TEXT_AT

VMEM_LIMIT = 48 * 1024 * 1024


def dot_f32(left, right):
    return lax.dot_general(
        left, right, (((1,), (0,)), ((), ())), preferred_element_type=jnp.float32
    )


def dot_t_f32(left, right):
    return lax.dot_general(
        left, right, (((1,), (1,)), ((), ())), preferred_element_type=jnp.float32
    )


def head_slot():
    return lax.axis_index("z") * 2 + lax.axis_index("yl")


def head_of(rank):
    slot = rank % 16
    return rank // 16 * PAIR_HEADS + slot if slot < PAIR_HEADS else None


def in_hbm(array):
    return pltpu.with_memory_space_constraint(array, pltpu.HBM)


def one_hot(condition):
    return jnp.where(condition, 1.0, 0.0).astype(jnp.bfloat16)


def message_of(source, rows):
    return (source * (65536 // rows + 1)) // 65536


def pack_kernel(
    k1, v1, q1, q2, k2, v2, text_k, text_v, gates, steps, out, extra,
    held, stacked, gate, step_ids, sems,
):
    slot = lax.rem(head_slot(), GROUP_HEADS)
    columns = pl.ds(pl.multiple_of(slot * HEAD_DIM, HEAD_DIM), HEAD_DIM)
    targets = [(array, held.at[index]) for index, array in enumerate((k1, v1, q1, q2, k2, v2))]
    targets += [
        (steps, step_ids),
        (gates.at[:, columns], gate),
        (text_k.at[:, columns], extra.at[pl.ds(0, TEXT)]),
        (text_v.at[:, columns], extra.at[pl.ds(TEXT, TEXT)]),
    ]
    fetches = [
        pltpu.make_async_copy(source, target, sems.at[index])
        for index, (source, target) in enumerate(targets)
    ]
    for fetch in fetches:
        fetch.start()
    stacked[...] = jnp.zeros_like(stacked)
    source = lax.broadcasted_iota(jnp.int32, (1, 8 * 48), 1)
    message = message_of(source, 48)
    array = (source - message * 48) // 8
    entry = source - message * 48 - array * 8
    target = jnp.where(entry < ROWS, message * CHUNK + array * ROWS + entry, -1)
    order = one_hot(lax.broadcasted_iota(jnp.int32, (8 * CHUNK, 8 * 48), 0) == target)
    for index in range(6):
        fetches[index].wait()
        stacked[pl.ds(index * 8, ROWS)] = held[index]
    for part in range(PEERS // 8):
        place = pl.ds(part * 8 * CHUNK, 8 * CHUNK)
        pieces = []
        for rank in range(part * 8, part * 8 + 8):
            head = head_of(rank)
            if head is None:
                pieces.append(jnp.zeros((48, HEAD_DIM), jnp.bfloat16))
            else:
                pieces.append(stacked[:, head * HEAD_DIM : (head + 1) * HEAD_DIM])
        out[place] = dot_f32(order, jnp.concatenate(pieces, axis=0)).astype(jnp.bfloat16)
    for fetch in fetches[6:]:
        fetch.wait()
    row = lax.broadcasted_iota(jnp.int32, (16, HEAD_DIM), 0)
    parts = jnp.zeros((16, HEAD_DIM), jnp.float32)
    for step in range(2):
        left = gate[pl.ds(step_ids[step], 1), :]
        for index in range(3):
            part = left.astype(jnp.bfloat16).astype(jnp.float32)
            parts = jnp.where(row == step * 3 + index, part, parts)
            left = left - part
    extra[pl.ds(2 * TEXT, 16)] = parts.astype(jnp.bfloat16)


def pack(*arrays):
    vmem = pl.BlockSpec(memory_space=pltpu.VMEM)
    return pl.pallas_call(
        pack_kernel,
        out_shape=(
            jax.ShapeDtypeStruct((PEERS * CHUNK, HEAD_DIM), jnp.bfloat16),
            jax.ShapeDtypeStruct((EXTRA, HEAD_DIM), jnp.bfloat16),
        ),
        in_specs=[pl.BlockSpec(memory_space=pltpu.HBM)] * 10,
        out_specs=(vmem, vmem),
        scratch_shapes=[
            pltpu.VMEM((6, ROWS, HEADS * HEAD_DIM), jnp.bfloat16),
            pltpu.VMEM((48, HEADS * HEAD_DIM), jnp.bfloat16),
            pltpu.VMEM((35, HEAD_DIM), jnp.float32),
            pltpu.SMEM((2,), jnp.int32),
            pltpu.SemaphoreType.DMA((10,)),
        ],
        compiler_params=pltpu.CompilerParams(vmem_limit_bytes=VMEM_LIMIT),
    )(*[in_hbm(array) for array in arrays])


def unpack_kernel(messages, copies, queries, near):
    source = lax.broadcasted_iota(jnp.int32, (1, 8 * CHUNK), 1)
    message = message_of(source, CHUNK)
    entry = source - message * CHUNK
    target = entry + ((entry * 13) // 64) * 35 + message * ROWS
    order = one_hot(lax.broadcasted_iota(jnp.int32, (240, 8 * CHUNK), 0) == target)
    for step in range(8):
        rows = messages[pl.ds(step * 8 * CHUNK, 8 * CHUNK)]
        ordered = dot_f32(order, rows).astype(jnp.bfloat16)
        for array in range(6):
            piece = ordered[array * 40 : (array + 1) * 40]
            place = pl.ds((array % 2) * PLANE_ROWS + step * 40, 40)
            if array < 2:
                for copy in range(4):
                    copies[copy, place] = piece
            elif array < 4:
                queries[place] = piece
            else:
                near[place] = piece


def unpack(messages):
    rows = jax.ShapeDtypeStruct((2 * PLANE_ROWS, HEAD_DIM), jnp.bfloat16)
    return pl.pallas_call(
        unpack_kernel,
        out_shape=(
            jax.ShapeDtypeStruct((4, 2 * PLANE_ROWS, HEAD_DIM), jnp.bfloat16),
            rows,
            rows,
        ),
        compiler_params=pltpu.CompilerParams(vmem_limit_bytes=VMEM_LIMIT),
    )(messages)


def join_kernel(planes, near, extra, out):
    own = lax.axis_index("x")
    for place in range(4):
        source = lax.rem(own + place, 4)
        for part in range(2):
            out[pl.ds(part * HALF + place * PLANE_ROWS, PLANE_ROWS)] = planes[
                source, pl.ds(part * PLANE_ROWS, PLANE_ROWS)
            ]
    out[pl.ds(NEAR_AT, 2 * PLANE_ROWS)] = near[...]
    out[pl.ds(TEXT_AT, EXTRA)] = extra[...]


def join(planes, near, extra):
    return pl.pallas_call(
        join_kernel,
        out_shape=jax.ShapeDtypeStruct((SHARED, HEAD_DIM), jnp.bfloat16),
        compiler_params=pltpu.CompilerParams(vmem_limit_bytes=VMEM_LIMIT),
    )(planes, near, extra)


TILE = 160
TILES = 2 * PLANE_ROWS // TILE
NEAR = 384
CUTS = ((0, 512), (512, 1024), (1024, HALF))


def floor_of(index, step):
    return jnp.floor((index + 0.5) * (1.0 / step))


def block_of(index):
    message = floor_of(index.astype(jnp.float32), ROWS)
    return message - 16.0 * floor_of(message, 16)


def beside_ones(target, rows):
    target[:, :HEAD_DIM] = rows
    target[:, HEAD_DIM:] = jnp.ones_like(rows)


def same_block(tile):
    row = lax.broadcasted_iota(jnp.int32, (TILE, 1), 0) + (tile * TILE) % PLANE_ROWS
    column = lax.broadcasted_iota(jnp.int32, (1, NEAR), 1)
    return block_of(row) == jnp.where(column < PLANE_ROWS, block_of(column), -1.0)


def tile_rows(tile):
    return pl.ds(tile * TILE, TILE)


def half_scores(queries, keys, tile, cut):
    rows = queries[tile_rows(tile)]
    scores = dot_t_f32(rows, keys[pl.ds(cut[0], cut[1] - cut[0])])
    if tile * TILE >= PLANE_ROWS and cut[0] == 0:
        near = dot_t_f32(rows, keys[pl.ds(NEAR_AT, NEAR)])
        near = jnp.where(same_block(tile), near, scores[:, :NEAR])
        scores = jnp.concatenate([near, scores[:, NEAR:]], axis=1)
    return scores


def half_sums(weights, values, near_values, tile, cut):
    part = values[pl.ds(cut[0], cut[1] - cut[0])]
    if tile * TILE >= PLANE_ROWS and cut[0] == 0:
        same = same_block(tile)
        local = weights[:, :NEAR]
        blank = jnp.zeros_like(local)
        far = jnp.concatenate([jnp.where(same, blank, local), weights[:, NEAR:]], axis=1)
        return dot_f32(far, part) + dot_f32(jnp.where(same, local, blank), near_values[...])
    return dot_f32(weights, part)


def lane_max(scores, former):
    for begin in range(0, scores.shape[1], HEAD_DIM):
        piece = scores[:, begin : begin + HEAD_DIM]
        former = piece if former is None else jnp.maximum(former, piece)
    return former


def weigh(scores, top):
    return jnp.exp2((scores - top) * EXP_SCALE).astype(jnp.bfloat16)


def run_tiles(score_parts, sum_parts, start_top, finish_tile):
    former = None
    for tile in range(TILES + 1):
        scores, lanes, sums = [], None, None
        for index in range(len(score_parts)):
            if tile < TILES:
                part = score_parts[index](tile)
                lanes = lane_max(part, lanes)
                scores.append(part)
            if former is not None:
                part = sum_parts[index](weigh(former[0][index], former[1]), tile - 1)
                sums = part if sums is None else sums + part
        if former is not None:
            finish_tile(tile - 1, former[1], sums)
        if tile < TILES:
            top = jnp.max(lanes, axis=1, keepdims=True)
            former = (scores, start_top(tile, top))


def first_kernel(queries, mine, sums, tops, values, near_values):
    beside_ones(values, mine[pl.ds(HALF, HALF)])
    beside_ones(near_values, mine[pl.ds(NEAR_AT + PLANE_ROWS, NEAR)])

    def finish_tile(tile, top, total):
        sums[tile_rows(tile)] = total
        tops[tile_rows(tile)] = jnp.broadcast_to(top, (TILE, HEAD_DIM))

    run_tiles(
        [lambda tile, cut=cut: half_scores(queries, mine, tile, cut) for cut in CUTS],
        [
            lambda weights, tile, cut=cut: half_sums(weights, values, near_values, tile, cut)
            for cut in CUTS
        ],
        lambda tile, top: top,
        finish_tile,
    )


def second_kernel(
    length, queries, mine, theirs, sums, tops, out, values, near_values, text, text_values, done
):
    here = head_slot() // GROUP_HEADS == lax.axis_index("c")

    @pl.when(here)
    def _():
        text[...] = mine[pl.ds(TEXT_AT, EXTRA)]

    @pl.when(jnp.logical_not(here))
    def _():
        text[...] = theirs[pl.ds(TEXT_AT, EXTRA)]

    beside_ones(values, theirs[pl.ds(HALF, HALF)])
    beside_ones(near_values, theirs[pl.ds(NEAR_AT + PLANE_ROWS, NEAR)])
    beside_ones(text_values, text[pl.ds(TEXT, TEXT)])
    parts = text[pl.ds(2 * TEXT, 16)].astype(jnp.float32)
    live = lax.broadcasted_iota(jnp.int32, (1, TEXT), 1) < length[0]

    def text_scores(tile):
        scores = dot_t_f32(queries[tile_rows(tile)], text[pl.ds(0, TEXT)])
        return jnp.where(live, scores, -1e30)

    def start_top(tile, top):
        return jnp.maximum(tops[tile_rows(tile), 0:1], top)

    def finish_tile(tile, top, total):
        former = jnp.exp2((tops[tile_rows(tile), 0:1] - top) * EXP_SCALE)
        total = total + sums[tile_rows(tile)] * former
        step = tile * TILE // PLANE_ROWS
        gate = parts[3 * step : 3 * step + 1] + parts[3 * step + 1 : 3 * step + 2]
        gate = gate + parts[3 * step + 2 : 3 * step + 3]
        attended = total[:, :HEAD_DIM] / total[:, HEAD_DIM:]
        done[tile_rows(tile)] = (gate * attended).astype(jnp.bfloat16)

    run_tiles(
        [lambda tile, cut=cut: half_scores(queries, theirs, tile, cut) for cut in CUTS]
        + [text_scores],
        [
            lambda weights, tile, cut=cut: half_sums(weights, values, near_values, tile, cut)
            for cut in CUTS
        ]
        + [lambda weights, tile: dot_f32(weights, text_values[...])],
        start_top,
        finish_tile,
    )
    row = lax.broadcasted_iota(jnp.int32, (160, 80), 0)
    column = lax.broadcasted_iota(jnp.int32, (160, 80), 1)
    place_first = one_hot(row == 2 * column)
    place_second = one_hot(row == 2 * column + 1)
    for part in range(4):
        rows = dot_f32(place_first, done[pl.ds(part * 80, 80)])
        rows += dot_f32(place_second, done[pl.ds(PLANE_ROWS + part * 80, 80)])
        out[pl.ds(part * 160, 160)] = rows.astype(jnp.bfloat16)


def first_pass(queries, mine):
    vmem = pl.BlockSpec(memory_space=pltpu.VMEM)
    return pl.pallas_call(
        first_kernel,
        out_shape=(
            jax.ShapeDtypeStruct((2 * PLANE_ROWS, 2 * HEAD_DIM), jnp.float32),
            jax.ShapeDtypeStruct((2 * PLANE_ROWS, HEAD_DIM), jnp.float32),
        ),
        in_specs=[vmem, vmem],
        out_specs=(vmem, vmem),
        scratch_shapes=[
            pltpu.VMEM((HALF, 2 * HEAD_DIM), jnp.bfloat16),
            pltpu.VMEM((NEAR, 2 * HEAD_DIM), jnp.bfloat16),
        ],
        cost_estimate=pl.CostEstimate(
            flops=4 * 640 * 1600 * HEAD_DIM, bytes_accessed=2 * SHARED * HEAD_DIM, transcendentals=640 * HALF
        ),
        compiler_params=pltpu.CompilerParams(vmem_limit_bytes=VMEM_LIMIT),
    )(queries, mine)


def second_pass(text_length, queries, mine, theirs, sums, tops):
    vmem = pl.BlockSpec(memory_space=pltpu.VMEM)
    return pl.pallas_call(
        second_kernel,
        out_shape=jax.ShapeDtypeStruct((PEERS * BACK, HEAD_DIM), jnp.bfloat16),
        in_specs=[pl.BlockSpec(memory_space=pltpu.SMEM)] + [vmem] * 5,
        out_specs=vmem,
        scratch_shapes=[
            pltpu.VMEM((HALF, 2 * HEAD_DIM), jnp.bfloat16),
            pltpu.VMEM((NEAR, 2 * HEAD_DIM), jnp.bfloat16),
            pltpu.VMEM((EXTRA, HEAD_DIM), jnp.bfloat16),
            pltpu.VMEM((TEXT, 2 * HEAD_DIM), jnp.bfloat16),
            pltpu.VMEM((2 * PLANE_ROWS, HEAD_DIM), jnp.bfloat16),
        ],
        compiler_params=pltpu.CompilerParams(vmem_limit_bytes=VMEM_LIMIT),
    )(text_length, queries, mine, theirs, sums, tops)


def finish_kernel(messages, first, second):
    source = lax.broadcasted_iota(jnp.int32, (1, 8 * BACK), 1)
    message = message_of(source, BACK)
    entry = source - message * BACK
    target = message * 16 + (entry % 2) * 8 + entry // 2
    order = one_hot(lax.broadcasted_iota(jnp.int32, (128, 8 * BACK), 0) == target)
    for part in range(PEERS // 8):
        rows = dot_f32(order, messages[pl.ds(part * 8 * BACK, 8 * BACK)]).astype(jnp.bfloat16)
        for index in range(8):
            rank = part * 8 + index
            head = head_of(rank)
            if head is None:
                continue
            columns = pl.ds(head * HEAD_DIM, HEAD_DIM)
            first[:, columns] = rows[index * 16 : index * 16 + ROWS]
            second[:, columns] = rows[index * 16 + 8 : index * 16 + 8 + ROWS]


def finish(messages):
    shape = jax.ShapeDtypeStruct((ROWS, HEADS * HEAD_DIM), jnp.bfloat16)
    return pl.pallas_call(
        finish_kernel,
        out_shape=(shape, shape),
        compiler_params=pltpu.CompilerParams(vmem_limit_bytes=VMEM_LIMIT),
    )(messages)


def body(
    query_first,
    keys_first,
    values_first,
    query_second,
    keys_second,
    values_second,
    text_keys,
    text_values,
    gate_table,
    timesteps,
    text_length,
):
    sent, extra = pack(
        keys_first,
        values_first,
        query_first,
        query_second,
        keys_second,
        values_second,
        text_keys,
        text_values,
        gate_table,
        timesteps,
    )
    pairs = sent.reshape(PEERS, CHUNK // 2, 2, HEAD_DIM)
    arrived = lax.all_to_all(pairs, PLANE, 0, 0, tiled=True)
    copies, queries, near = unpack(arrived.reshape(PEERS * CHUNK, HEAD_DIM))
    planes = lax.all_to_all(copies, "x", 0, 0, tiled=True)
    mine = join(planes, near, extra)
    theirs = lax.ppermute(mine, "c", [(0, 1), (1, 0)])
    sums, tops = first_pass(queries, mine)
    back = second_pass(text_length, queries, mine, theirs, sums, tops)
    pairs = back.reshape(PEERS, ROWS, 2, HEAD_DIM)
    returned = lax.all_to_all(pairs, PLANE, 0, 0, tiled=True)
    return finish(returned.reshape(PEERS * BACK, HEAD_DIM))


def solution(mesh):
    fine = Mesh(mesh.devices.reshape(8, 4, 2, 4, 2), AXES)
    rows = P(AXES, None)
    heads = P(None, ("yh", "c"))
    return jax.shard_map(
        body,
        mesh=fine,
        in_specs=(rows,) * 6 + (heads,) * 3 + (P(), P()),
        out_specs=(rows, rows),
        check_vma=False,
    )
```

```python
import jax
import jax.numpy as jnp
import numpy as np
from jax import lax
from jax.experimental import pallas as pl
from jax.experimental.pallas import tpu as pltpu
from jax.sharding import Mesh
from jax.sharding import PartitionSpec as P

HEAD_DIM = 128
HEADS = 40
GROUP_HEADS = 5
PAIR_HEADS = 10
ROWS = 5
PLANE_ROWS = 320
PEERS = 64
CHUNK = 6 * ROWS
BACK = 2 * ROWS
TEXT = 512
EXP_SCALE = float(HEAD_DIM ** (-0.5) * np.log2(np.e))

AXES = ("z", "x", "yl", "yh", "c")
PLANE = ("yh", "z", "yl")

HALF = 4 * PLANE_ROWS
NEAR_AT = 2 * HALF
TEXT_AT = NEAR_AT + 2 * PLANE_ROWS
GATE_AT = TEXT_AT + 2 * TEXT
SHARED = GATE_AT + 16
EXTRA = SHARED - TEXT_AT

VMEM_LIMIT = 48 * 1024 * 1024


def dot_f32(left, right):
    return lax.dot_general(
        left, right, (((1,), (0,)), ((), ())), preferred_element_type=jnp.float32
    )


def dot_t_f32(left, right):
    return lax.dot_general(
        left, right, (((1,), (1,)), ((), ())), preferred_element_type=jnp.float32
    )


def head_slot():
    return lax.axis_index("z") * 2 + lax.axis_index("yl")


def head_of(rank):
    slot = rank % 16
    return rank // 16 * PAIR_HEADS + slot if slot < PAIR_HEADS else None


def in_hbm(array):
    return pltpu.with_memory_space_constraint(array, pltpu.HBM)


def one_hot(condition):
    return jnp.where(condition, 1.0, 0.0).astype(jnp.bfloat16)


def message_of(source, rows):
    return (source * (65536 // rows + 1)) // 65536


def pack_kernel(
    k1, v1, q1, q2, k2, v2, text_k, text_v, gates, steps, out, extra,
    held, stacked, gate, step_ids, sems,
):
    slot = lax.rem(head_slot(), GROUP_HEADS)
    columns = pl.ds(pl.multiple_of(slot * HEAD_DIM, HEAD_DIM), HEAD_DIM)
    targets = [(array, held.at[index]) for index, array in enumerate((k1, v1, q1, q2, k2, v2))]
    targets += [
        (steps, step_ids),
        (gates.at[:, columns], gate),
        (text_k.at[:, columns], extra.at[pl.ds(0, TEXT)]),
        (text_v.at[:, columns], extra.at[pl.ds(TEXT, TEXT)]),
    ]
    fetches = [
        pltpu.make_async_copy(source, target, sems.at[index])
        for index, (source, target) in enumerate(targets)
    ]
    for fetch in fetches:
        fetch.start()
    stacked[...] = jnp.zeros_like(stacked)
    source = lax.broadcasted_iota(jnp.int32, (1, 8 * 48), 1)
    message = message_of(source, 48)
    array = (source - message * 48) // 8
    entry = source - message * 48 - array * 8
    target = jnp.where(entry < ROWS, message * CHUNK + array * ROWS + entry, -1)
    order = one_hot(lax.broadcasted_iota(jnp.int32, (8 * CHUNK, 8 * 48), 0) == target)
    for index in range(6):
        fetches[index].wait()
        stacked[pl.ds(index * 8, ROWS)] = held[index]
    for part in range(PEERS // 8):
        place = pl.ds(part * 8 * CHUNK, 8 * CHUNK)
        pieces = []
        for rank in range(part * 8, part * 8 + 8):
            head = head_of(rank)
            if head is None:
                pieces.append(jnp.zeros((48, HEAD_DIM), jnp.bfloat16))
            else:
                pieces.append(stacked[:, head * HEAD_DIM : (head + 1) * HEAD_DIM])
        out[place] = dot_f32(order, jnp.concatenate(pieces, axis=0)).astype(jnp.bfloat16)
    for fetch in fetches[6:]:
        fetch.wait()
    row = lax.broadcasted_iota(jnp.int32, (16, HEAD_DIM), 0)
    parts = jnp.zeros((16, HEAD_DIM), jnp.float32)
    for step in range(2):
        left = gate[pl.ds(step_ids[step], 1), :]
        for index in range(3):
            part = left.astype(jnp.bfloat16).astype(jnp.float32)
            parts = jnp.where(row == step * 3 + index, part, parts)
            left = left - part
    extra[pl.ds(2 * TEXT, 16)] = parts.astype(jnp.bfloat16)


def pack(*arrays):
    vmem = pl.BlockSpec(memory_space=pltpu.VMEM)
    return pl.pallas_call(
        pack_kernel,
        out_shape=(
            jax.ShapeDtypeStruct((PEERS * CHUNK, HEAD_DIM), jnp.bfloat16),
            jax.ShapeDtypeStruct((EXTRA, HEAD_DIM), jnp.bfloat16),
        ),
        in_specs=[pl.BlockSpec(memory_space=pltpu.HBM)] * 10,
        out_specs=(vmem, vmem),
        scratch_shapes=[
            pltpu.VMEM((6, ROWS, HEADS * HEAD_DIM), jnp.bfloat16),
            pltpu.VMEM((48, HEADS * HEAD_DIM), jnp.bfloat16),
            pltpu.VMEM((35, HEAD_DIM), jnp.float32),
            pltpu.SMEM((2,), jnp.int32),
            pltpu.SemaphoreType.DMA((10,)),
        ],
        compiler_params=pltpu.CompilerParams(vmem_limit_bytes=VMEM_LIMIT),
    )(*[in_hbm(array) for array in arrays])


def unpack_kernel(messages, plane, queries, near):
    source = lax.broadcasted_iota(jnp.int32, (1, 8 * CHUNK), 1)
    message = message_of(source, CHUNK)
    entry = source - message * CHUNK
    target = entry + ((entry * 13) // 64) * 35 + message * ROWS
    order = one_hot(lax.broadcasted_iota(jnp.int32, (240, 8 * CHUNK), 0) == target)
    for step in range(8):
        rows = messages[pl.ds(step * 8 * CHUNK, 8 * CHUNK)]
        ordered = dot_f32(order, rows).astype(jnp.bfloat16)
        for array in range(6):
            piece = ordered[array * 40 : (array + 1) * 40]
            place = pl.ds((array % 2) * PLANE_ROWS + step * 40, 40)
            if array < 2:
                plane[place] = piece
            elif array < 4:
                queries[place] = piece
            else:
                near[place] = piece


def unpack(messages):
    rows = jax.ShapeDtypeStruct((2 * PLANE_ROWS, HEAD_DIM), jnp.bfloat16)
    return pl.pallas_call(
        unpack_kernel,
        out_shape=(
            rows,
            rows,
            rows,
        ),
        compiler_params=pltpu.CompilerParams(vmem_limit_bytes=VMEM_LIMIT),
    )(messages)


def join_kernel(*refs):
    planes, (near, extra, out) = refs[:4], refs[4:]
    for place, plane in enumerate(planes):
        for part in range(2):
            out[pl.ds(part * HALF + place * PLANE_ROWS, PLANE_ROWS)] = plane[
                pl.ds(part * PLANE_ROWS, PLANE_ROWS)
            ]
    out[pl.ds(NEAR_AT, 2 * PLANE_ROWS)] = near[...]
    out[pl.ds(TEXT_AT, EXTRA)] = extra[...]


def join(planes, near, extra):
    return pl.pallas_call(
        join_kernel,
        out_shape=jax.ShapeDtypeStruct((SHARED, HEAD_DIM), jnp.bfloat16),
        compiler_params=pltpu.CompilerParams(vmem_limit_bytes=VMEM_LIMIT),
    )(*planes, near, extra)


TILE = 160
TILES = 2 * PLANE_ROWS // TILE
NEAR = 384
CUTS = ((0, 512), (512, 1024), (1024, HALF))


def floor_of(index, step):
    return jnp.floor((index + 0.5) * (1.0 / step))


def block_of(index):
    message = floor_of(index.astype(jnp.float32), ROWS)
    return message - 16.0 * floor_of(message, 16)


def beside_ones(target, rows):
    target[:, :HEAD_DIM] = rows
    target[:, HEAD_DIM:] = jnp.ones_like(rows)


def same_block(tile):
    row = lax.broadcasted_iota(jnp.int32, (TILE, 1), 0) + (tile * TILE) % PLANE_ROWS
    column = lax.broadcasted_iota(jnp.int32, (1, NEAR), 1)
    return block_of(row) == jnp.where(column < PLANE_ROWS, block_of(column), -1.0)


def tile_rows(tile):
    return pl.ds(tile * TILE, TILE)


def half_scores(queries, keys, tile, cut):
    rows = queries[tile_rows(tile)]
    scores = dot_t_f32(rows, keys[pl.ds(cut[0], cut[1] - cut[0])])
    if tile * TILE >= PLANE_ROWS and cut[0] == 0:
        near = dot_t_f32(rows, keys[pl.ds(NEAR_AT, NEAR)])
        near = jnp.where(same_block(tile), near, scores[:, :NEAR])
        scores = jnp.concatenate([near, scores[:, NEAR:]], axis=1)
    return scores


def half_sums(weights, values, near_values, tile, cut):
    part = values[pl.ds(cut[0], cut[1] - cut[0])]
    if tile * TILE >= PLANE_ROWS and cut[0] == 0:
        same = same_block(tile)
        local = weights[:, :NEAR]
        blank = jnp.zeros_like(local)
        far = jnp.concatenate([jnp.where(same, blank, local), weights[:, NEAR:]], axis=1)
        return dot_f32(far, part) + dot_f32(jnp.where(same, local, blank), near_values[...])
    return dot_f32(weights, part)


def lane_max(scores, former):
    for begin in range(0, scores.shape[1], HEAD_DIM):
        piece = scores[:, begin : begin + HEAD_DIM]
        former = piece if former is None else jnp.maximum(former, piece)
    return former


def weigh(scores, top):
    return jnp.exp2((scores - top) * EXP_SCALE).astype(jnp.bfloat16)


def run_tiles(score_parts, sum_parts, start_top, finish_tile):
    former = None
    for tile in range(TILES + 1):
        scores, lanes, sums = [], None, None
        for index in range(len(score_parts)):
            if tile < TILES:
                part = score_parts[index](tile)
                lanes = lane_max(part, lanes)
                scores.append(part)
            if former is not None:
                part = sum_parts[index](weigh(former[0][index], former[1]), tile - 1)
                sums = part if sums is None else sums + part
        if former is not None:
            finish_tile(tile - 1, former[1], sums)
        if tile < TILES:
            top = jnp.max(lanes, axis=1, keepdims=True)
            former = (scores, start_top(tile, top))


def first_kernel(queries, mine, sums, tops, values, near_values):
    beside_ones(values, mine[pl.ds(HALF, HALF)])
    beside_ones(near_values, mine[pl.ds(NEAR_AT + PLANE_ROWS, NEAR)])

    def finish_tile(tile, top, total):
        sums[tile_rows(tile)] = total
        tops[tile_rows(tile)] = jnp.broadcast_to(top, (TILE, HEAD_DIM))

    run_tiles(
        [lambda tile, cut=cut: half_scores(queries, mine, tile, cut) for cut in CUTS],
        [
            lambda weights, tile, cut=cut: half_sums(weights, values, near_values, tile, cut)
            for cut in CUTS
        ],
        lambda tile, top: top,
        finish_tile,
    )


def second_kernel(
    length, queries, mine, theirs, sums, tops, out, values, near_values, text, text_values, done
):
    here = head_slot() // GROUP_HEADS == lax.axis_index("c")

    @pl.when(here)
    def _():
        text[...] = mine[pl.ds(TEXT_AT, EXTRA)]

    @pl.when(jnp.logical_not(here))
    def _():
        text[...] = theirs[pl.ds(TEXT_AT, EXTRA)]

    beside_ones(values, theirs[pl.ds(HALF, HALF)])
    beside_ones(near_values, theirs[pl.ds(NEAR_AT + PLANE_ROWS, NEAR)])
    beside_ones(text_values, text[pl.ds(TEXT, TEXT)])
    parts = text[pl.ds(2 * TEXT, 16)].astype(jnp.float32)
    live = lax.broadcasted_iota(jnp.int32, (1, TEXT), 1) < length[0]

    def text_scores(tile):
        scores = dot_t_f32(queries[tile_rows(tile)], text[pl.ds(0, TEXT)])
        return jnp.where(live, scores, -1e30)

    def start_top(tile, top):
        return jnp.maximum(tops[tile_rows(tile), 0:1], top)

    def finish_tile(tile, top, total):
        former = jnp.exp2((tops[tile_rows(tile), 0:1] - top) * EXP_SCALE)
        total = total + sums[tile_rows(tile)] * former
        step = tile * TILE // PLANE_ROWS
        gate = parts[3 * step : 3 * step + 1] + parts[3 * step + 1 : 3 * step + 2]
        gate = gate + parts[3 * step + 2 : 3 * step + 3]
        attended = total[:, :HEAD_DIM] / total[:, HEAD_DIM:]
        done[tile_rows(tile)] = (gate * attended).astype(jnp.bfloat16)

    run_tiles(
        [lambda tile, cut=cut: half_scores(queries, theirs, tile, cut) for cut in CUTS]
        + [text_scores],
        [
            lambda weights, tile, cut=cut: half_sums(weights, values, near_values, tile, cut)
            for cut in CUTS
        ]
        + [lambda weights, tile: dot_f32(weights, text_values[...])],
        start_top,
        finish_tile,
    )
    row = lax.broadcasted_iota(jnp.int32, (160, 80), 0)
    column = lax.broadcasted_iota(jnp.int32, (160, 80), 1)
    place_first = one_hot(row == 2 * column)
    place_second = one_hot(row == 2 * column + 1)
    for part in range(4):
        rows = dot_f32(place_first, done[pl.ds(part * 80, 80)])
        rows += dot_f32(place_second, done[pl.ds(PLANE_ROWS + part * 80, 80)])
        out[pl.ds(part * 160, 160)] = rows.astype(jnp.bfloat16)


def first_pass(queries, mine):
    vmem = pl.BlockSpec(memory_space=pltpu.VMEM)
    return pl.pallas_call(
        first_kernel,
        out_shape=(
            jax.ShapeDtypeStruct((2 * PLANE_ROWS, 2 * HEAD_DIM), jnp.float32),
            jax.ShapeDtypeStruct((2 * PLANE_ROWS, HEAD_DIM), jnp.float32),
        ),
        in_specs=[vmem, vmem],
        out_specs=(vmem, vmem),
        scratch_shapes=[
            pltpu.VMEM((HALF, 2 * HEAD_DIM), jnp.bfloat16),
            pltpu.VMEM((NEAR, 2 * HEAD_DIM), jnp.bfloat16),
        ],
        cost_estimate=pl.CostEstimate(
            flops=4 * 640 * 1600 * HEAD_DIM, bytes_accessed=2 * SHARED * HEAD_DIM, transcendentals=640 * HALF
        ),
        compiler_params=pltpu.CompilerParams(vmem_limit_bytes=VMEM_LIMIT),
    )(queries, mine)


def second_pass(text_length, queries, mine, theirs, sums, tops):
    vmem = pl.BlockSpec(memory_space=pltpu.VMEM)
    return pl.pallas_call(
        second_kernel,
        out_shape=jax.ShapeDtypeStruct((PEERS * BACK, HEAD_DIM), jnp.bfloat16),
        in_specs=[pl.BlockSpec(memory_space=pltpu.SMEM)] + [vmem] * 5,
        out_specs=vmem,
        scratch_shapes=[
            pltpu.VMEM((HALF, 2 * HEAD_DIM), jnp.bfloat16),
            pltpu.VMEM((NEAR, 2 * HEAD_DIM), jnp.bfloat16),
            pltpu.VMEM((EXTRA, HEAD_DIM), jnp.bfloat16),
            pltpu.VMEM((TEXT, 2 * HEAD_DIM), jnp.bfloat16),
            pltpu.VMEM((2 * PLANE_ROWS, HEAD_DIM), jnp.bfloat16),
        ],
        compiler_params=pltpu.CompilerParams(vmem_limit_bytes=VMEM_LIMIT),
    )(text_length, queries, mine, theirs, sums, tops)


def finish_kernel(messages, first, second):
    source = lax.broadcasted_iota(jnp.int32, (1, 8 * BACK), 1)
    message = message_of(source, BACK)
    entry = source - message * BACK
    target = message * 16 + (entry % 2) * 8 + entry // 2
    order = one_hot(lax.broadcasted_iota(jnp.int32, (128, 8 * BACK), 0) == target)
    for part in range(PEERS // 8):
        rows = dot_f32(order, messages[pl.ds(part * 8 * BACK, 8 * BACK)]).astype(jnp.bfloat16)
        for index in range(8):
            rank = part * 8 + index
            head = head_of(rank)
            if head is None:
                continue
            columns = pl.ds(head * HEAD_DIM, HEAD_DIM)
            first[:, columns] = rows[index * 16 : index * 16 + ROWS]
            second[:, columns] = rows[index * 16 + 8 : index * 16 + 8 + ROWS]


def finish(messages):
    shape = jax.ShapeDtypeStruct((ROWS, HEADS * HEAD_DIM), jnp.bfloat16)
    return pl.pallas_call(
        finish_kernel,
        out_shape=(shape, shape),
        compiler_params=pltpu.CompilerParams(vmem_limit_bytes=VMEM_LIMIT),
    )(messages)


def body(
    query_first,
    keys_first,
    values_first,
    query_second,
    keys_second,
    values_second,
    text_keys,
    text_values,
    gate_table,
    timesteps,
    text_length,
):
    sent, extra = pack(
        keys_first,
        values_first,
        query_first,
        query_second,
        keys_second,
        values_second,
        text_keys,
        text_values,
        gate_table,
        timesteps,
    )
    pairs = sent.reshape(PEERS, CHUNK // 2, 2, HEAD_DIM)
    arrived = lax.all_to_all(pairs, PLANE, 0, 0, tiled=True)
    plane, queries, near = unpack(arrived.reshape(PEERS * CHUNK, HEAD_DIM))
    planes = [plane] + [
        lax.ppermute(plane, "x", [((place + step) % 4, place) for place in range(4)])
        for step in (2, 1, 3)
    ]
    mine = join(planes, near, extra)
    theirs = lax.ppermute(mine, "c", [(0, 1), (1, 0)])
    sums, tops = first_pass(queries, mine)
    back = second_pass(text_length, queries, mine, theirs, sums, tops)
    pairs = back.reshape(PEERS, ROWS, 2, HEAD_DIM)
    returned = lax.all_to_all(pairs, PLANE, 0, 0, tiled=True)
    return finish(returned.reshape(PEERS * BACK, HEAD_DIM))


def solution(mesh):
    fine = Mesh(mesh.devices.reshape(8, 4, 2, 4, 2), AXES)
    rows = P(AXES, None)
    heads = P(None, ("yh", "c"))
    return jax.shard_map(
        body,
        mesh=fine,
        in_specs=(rows,) * 6 + (heads,) * 3 + (P(), P()),
        out_specs=(rows, rows),
        check_vma=False,
    )
```
